32 devices in a mesh: tile: 8 (over z, y), group: 4 (over x, core).
Axes of the slice: x: 2, y: 2, z: 4, core: 2. Of those that a mesh axis runs over, the one named last changes fastest.
Arguments:
- tracers: float32 [32, 16, 64, 256], P('group', None, 'tile'), may hold values from -6 to 6
- emissions: float32 [32, 64, 256], P('group', 'tile'), may hold values from -6 to 6
- winds: float32 [4, 2, 16, 64, 256], P('group', None, None, 'tile'), may hold values from -1.44 to 1.44, as said below
- diffusivity: float32 [4, 15, 64, 256], P('group', None, 'tile'), may hold values from 0.05 to 2
- substeps: int32 [8], replicated, may hold values from 1 to 6, as said below
- loader: int32 [8], replicated, may hold values from 0 to 3
Outputs:
- mixed: float32 [32, 16, 64, 256], P('group', None, 'tile')
The draws below stay inside these ranges and needn't reach their ends.
Inputs may be any that keep to these rules, and one draw needn't show every extreme that they name: The first and the last tile take 6 substeps. `winds`: divided by the substep count of the tile that holds the face (for a meridional value on a tile's first row, by the smaller count of that tile and the tile south of it), every entry lies within -0.24 to 0.24.
All inputs are finite; a program needn't handle non-finite values.
Results may differ from the reference program's by a relative error of at most 0.00002.
Values sent between devices are 32-bit elements; how exact they have to be, the bound alone decides.
No kernel may reach another device: no remote copies, remote signals or barrier semaphores. Data moves between devices by JAX's collectives and lax.ppermute only.
A program may use at most 64 MiB of HBM per device.

```python
import math
import jax
import jax.numpy as jnp
from jax import lax

TR_DEV = 8
LEV = 16
LAT_DEV = 8
LON = 256
ROUNDS = 6
TRACERS = 32
LAT = 64
TILES = 8
SLOTS = 4
N_GROUP = 4


def tile_counts(key):
    counts = jax.random.randint(jax.random.fold_in(key, 7), (TILES,), 1, ROUNDS + 1)
    position = jnp.arange(TILES)
    polar = (position == 0) | (position == TILES - 1)
    return jnp.where(polar, ROUNDS, counts).astype(jnp.int32)


def draw_substeps(key, part):
    return tile_counts(key)


def draw_winds(key, part):
    counts = tile_counts(key)
    row_index = jnp.arange(LAT)
    row_tiles = row_index // LAT_DEV
    own_count = counts[row_tiles]
    below_count = counts[jnp.maximum(row_tiles - 1, 0)]
    first_row = row_index % LAT_DEV == 0
    merid_count = jnp.where(first_row, jnp.minimum(own_count, below_count), own_count)
    row_scale = jnp.stack([own_count, merid_count]).astype(jnp.float32)
    draw_shape = (SLOTS, 2, LEV, LAT, LON)
    base_draw = jax.random.uniform(jax.random.fold_in(key, 19), draw_shape, jnp.float32, -0.24, 0.24)
    return (base_draw * row_scale[None, :, None, :, None]).astype(jnp.float32)


def plant(array, own_key, least, largest):
    extent = array.shape
    index_at = [jax.random.randint(jax.random.fold_in(own_key, axis), (), 0, extent[axis]) for axis in range(len(extent))]
    array = array.at[tuple(index_at)].set(least)
    longest = extent.index(max(extent))
    index_at[longest] = (index_at[longest] + 1) % extent[longest]
    return array.at[tuple(index_at)].set(largest)


def shard_levels(key, shape, pieces, least, largest):
    level = 1.0
    for axis_at, shards_of in pieces:
        steps = jax.random.uniform(jax.random.fold_in(jax.random.fold_in(key, 6), axis_at), (shards_of,), jnp.float32, least / len(pieces), largest / len(pieces))
        level = level * jnp.repeat(jnp.exp(steps), shape[axis_at] // shards_of).reshape((-1,) + (1,) * (len(shape) - 1 - axis_at))
    return level


def noise(rng, shape, spread, most, split=(), held_as=jnp.bfloat16):
    gain = shard_levels(rng, shape, split, -0.22, 0.18) if split else 1.0
    array = jax.random.normal(rng, shape, jnp.float32) * spread * gain
    return jnp.minimum(jnp.maximum(array, -most), most).astype(held_as)


def setup_inputs(seed: int = 0) -> dict:
    key_list = jax.random.split(jax.random.key(seed), 7)
    tracers = noise(key_list[0], (TRACERS, LEV, LAT, LON), 1.0, 6.0, ((0, 4), (2, 8)), jnp.float32)
    emissions = noise(key_list[1], (TRACERS, LAT, LON), 1.0, 6.0, ((0, 4), (1, 8)), jnp.float32)
    winds = draw_winds(jax.random.fold_in(key_list[6], 71), 0)
    diffusivity = jnp.clip(jnp.exp(math.log(2.0) - 3.6888794 * jax.random.uniform(key_list[3], (SLOTS, LEV - 1, LAT, LON), jnp.float32) ** shard_levels(key_list[3], (SLOTS, LEV - 1, LAT, LON), ((0, 4), (2, 8)), -0.2, 0.2)), 0.05, 2.0)
    substeps = draw_substeps(jax.random.fold_in(key_list[6], 71), 0)
    loader = plant(jax.random.randint(key_list[5], (TILES,), 0, N_GROUP), jax.random.fold_in(key_list[5], 1), 0, N_GROUP - 1).astype(jnp.int32)
    return dict(tracers=tracers, emissions=emissions, winds=winds, diffusivity=diffusivity, substeps=substeps, loader=loader)


def thomas_solve(mixing, coefficient):
    levels = mixing.shape[1]
    zero_plane = jnp.zeros_like(coefficient[0])
    previous_ratio = zero_plane
    previous_value = jnp.zeros_like(mixing[:, 0])
    ratios = []
    values = []
    for level in range(levels):
        lower_coef = coefficient[level - 1] if level > 0 else zero_plane
        upper_coef = coefficient[level] if level < levels - 1 else zero_plane
        pivot = 1.0 / (1.0 + lower_coef + upper_coef - lower_coef * previous_ratio)
        previous_ratio = upper_coef * pivot
        previous_value = (mixing[:, level] + lower_coef * previous_value) * pivot
        ratios.append(previous_ratio)
        values.append(previous_value)
    solved = [None] * levels
    current = values[levels - 1]
    solved[levels - 1] = current
    for level in range(levels - 2, -1, -1):
        current = values[level] + ratios[level] * current
        solved[level] = current
    return jnp.stack(solved, axis=1)


def advance(mixing, zonal, meridional, fraction):
    from_west = jnp.roll(mixing, 1, axis=3)
    west_flux = jnp.maximum(zonal, 0.0) * from_west + jnp.minimum(zonal, 0.0) * mixing
    east_flux = jnp.roll(west_flux, -1, axis=3)
    zeros_row = jnp.zeros_like(mixing[:, :, :1])
    from_south = jnp.concatenate([zeros_row, mixing[:, :, :-1]], axis=2)
    south_flux = jnp.maximum(meridional, 0.0) * from_south + jnp.minimum(meridional, 0.0) * mixing
    north_flux = jnp.concatenate([south_flux[:, :, 1:], zeros_row], axis=2)
    return mixing - fraction[:, None] * ((east_flux - west_flux) + (north_flux - south_flux))


def reference(tracers, emissions, winds, diffusivity, substeps, loader):
    row_slots = jnp.repeat(loader.astype(jnp.int32), LAT_DEV)
    chosen = jnp.arange(SLOTS, dtype=jnp.int32)[:, None] == row_slots[None, :]
    courant = jnp.sum(jnp.where(chosen[:, None, None, :, None], winds, jnp.zeros_like(winds)), axis=0)
    coefficient = jnp.sum(jnp.where(chosen[:, None, :, None], diffusivity, jnp.zeros_like(diffusivity)), axis=0)
    row_index = jnp.arange(LAT)
    zonal = courant[0]
    meridional = courant[1] * (row_index > 0).astype(courant.dtype)[:, None]
    counts = jnp.repeat(substeps, LAT_DEV)
    counts_float = counts.astype(tracers.dtype)
    blocks = tracers.reshape(N_GROUP, TR_DEV, LEV, LAT, LON)
    sources = emissions.reshape(N_GROUP, TR_DEV, LAT, LON)

    def window(pair):
        mixing, source = pair
        for substep in range(ROUNDS):
            fraction = jnp.where(substep < counts, 1.0 / counts_float, jnp.zeros_like(counts_float))
            mixing = advance(mixing, zonal, meridional, fraction)
        mixing = mixing.at[:, 0].add(source)
        return thomas_solve(mixing, coefficient)

    result = lax.map(window, (blocks, sources))
    return result.reshape(TRACERS, LEV, LAT, LON)
```

```python
import functools

import jax
import jax.numpy as jnp
from jax import lax
from jax.experimental import pallas as pl
from jax.experimental.pallas import tpu as pltpu
from jax.sharding import PartitionSpec as P

ROUNDS = 6
PARTS = ((2, "relay"), (2, "relay"), (2, "relay"), (1, "relay"), (1, "straight"))
TOGETHER = 4


def exchange(value, axis, bit):
    count = lax.axis_size(axis)
    return lax.ppermute(value, axis, [(i, i ^ bit) for i in range(count)])


def shift(value, axis, by):
    count = lax.axis_size(axis)
    return lax.ppermute(value, axis, [(i, i + by) for i in range(count) if 0 <= i + by < count])


def relay(value, axis):
    count = lax.axis_size(axis)
    pairs = [(i, i + 2) for i in range(0, count - 2, 2)] + [(i, i - 2) for i in range(3, count, 2)]
    return lax.ppermute(value, axis, pairs)


def window_kernel(
    parts, has_prior, scalars, own, pair, far, wind_own, wind_pair, wind_far, mixing_coef, source, *rest
):
    if has_prior:
        rest = rest[1:]
    out, coef, values, ratios = rest
    tracers, levels, height, width = own.shape
    rows = 3 * height
    even = scalars[3] == 1
    first = scalars[4] == 1
    counts = [scalars[0], scalars[1], scalars[2]]

    def band(per_tile, dtype):
        return jnp.concatenate([jnp.full((height, width), c, dtype) for c in per_tile], axis=0)

    def stacked(middle, near, distant):
        south = jnp.where(even, distant, near)
        north = jnp.where(even, near, distant)
        return jnp.concatenate([south, middle, north], axis=0)

    ones = jnp.ones((height, width), jnp.float32)
    fraction = jnp.concatenate([ones / (ones * c.astype(jnp.float32)) for c in counts], axis=0)
    row = lax.broadcasted_iota(jnp.int32, (height, width), 0)
    pole = jnp.logical_and(row == 0, first)

    def prepare(level, carry):
        zonal = stacked(wind_own[0, level], wind_pair[0, level], wind_far[0, level])
        meridional = stacked(
            jnp.where(pole, 0.0, wind_own[1, level]), wind_pair[1, level], wind_far[1, level]
        )
        plus, minus = jnp.maximum(zonal, 0.0), jnp.minimum(zonal, 0.0)
        plus_east, minus_east = pltpu.roll(plus, width - 1, 1), pltpu.roll(minus, width - 1, 1)
        up, down = jnp.maximum(meridional, 0.0), jnp.minimum(meridional, 0.0)
        up_north, down_north = pltpu.roll(up, rows - 1, 0), pltpu.roll(down, rows - 1, 0)
        coef[level, 0] = 1.0 - fraction * ((plus_east - minus) + (up_north - down))
        coef[level, 1] = fraction * plus
        coef[level, 2] = -fraction * minus_east
        coef[level, 3] = fraction * up
        coef[level, 4] = -fraction * down_north
        return carry

    lax.fori_loop(0, levels, prepare, 0)

    count_rows = band(counts, jnp.int32)
    active = [count_rows > step for step in range(ROUNDS)]
    per = min(levels, max(1, TOGETHER // tracers))

    def advance(block, carry):
        previous_coef, previous_ratio, previous_values = carry
        fields = {}
        for k in range(per):
            level = block * per + k
            for n in range(tracers):
                fields[k, n] = stacked(own[n, level], pair[n, level], far[n, level])
        for step in range(ROUNDS):
            for k in range(per):
                level = block * per + k
                for n in range(tracers):
                    q = fields[k, n]
                    new = (
                        coef[level, 0] * q
                        + coef[level, 1] * pltpu.roll(q, 1, 1)
                        + coef[level, 2] * pltpu.roll(q, width - 1, 1)
                        + coef[level, 3] * pltpu.roll(q, 1, 0)
                        + coef[level, 4] * pltpu.roll(q, rows - 1, 0)
                    )
                    fields[k, n] = jnp.where(active[step], new, q)
        for k in range(per):
            level = block * per + k
            upper = jnp.where(level < levels - 1, mixing_coef[jnp.minimum(level, levels - 2)], 0.0)
            pivot = 1.0 / (1.0 + previous_coef + upper - previous_coef * previous_ratio)
            ratio = upper * pivot
            ratios[level] = ratio
            solved = []
            for n in range(tracers):
                q = fields[k, n][height : 2 * height]
                q = q + jnp.where(level == 0, source[n], 0.0)
                value = (q + previous_coef * previous_values[n]) * pivot
                values[n, level] = value
                solved.append(value)
            previous_coef, previous_ratio, previous_values = upper, ratio, tuple(solved)
        return previous_coef, previous_ratio, previous_values

    zero = jnp.zeros((height, width), jnp.float32)
    _, _, current = lax.fori_loop(0, levels // per, advance, (zero, zero, (zero,) * tracers))
    for n in range(tracers):
        out[n, levels - 1] = current[n]

    def back(step, current):
        level = levels - 2 - step
        ratio = ratios[level]
        solved = []
        for n in range(tracers):
            value = values[n, level] + ratio * current[n]
            out[n, level] = value
            solved.append(value)
        return tuple(solved)

    lax.fori_loop(0, levels - 1, back, current)


def window(scalars, tracers, emissions, start, count, pair, far, winds, mixing_coef, prior):
    levels, height, width = tracers.shape[1:]
    whole = pl.BlockSpec(memory_space=pltpu.VMEM)
    at = start // count
    part = pl.BlockSpec((count, levels, height, width), lambda i: (at, 0, 0, 0))
    in_specs = [
        pl.BlockSpec(memory_space=pltpu.SMEM),
        part,
        whole,
        whole,
        whole,
        whole,
        whole,
        whole,
        pl.BlockSpec((count, height, width), lambda i: (at, 0, 0)),
    ]
    operands = [scalars, tracers, pair, far, *winds, mixing_coef, emissions]
    if prior is not None:
        in_specs.append(pl.BlockSpec(memory_space=pl.ANY))
        operands.append(prior)
    cost = count * levels * height * width * 3 * ROUNDS * 16
    return pl.pallas_call(
        functools.partial(window_kernel, None, prior is not None),
        grid=(1,),
        out_shape=jax.ShapeDtypeStruct(tracers.shape, tracers.dtype),
        in_specs=in_specs,
        out_specs=part,
        scratch_shapes=[
            pltpu.VMEM((levels, 5, 3 * height, width), jnp.float32),
            pltpu.VMEM((count, levels, height, width), jnp.float32),
            pltpu.VMEM((levels, height, width), jnp.float32),
        ],
        input_output_aliases={} if prior is None else {len(operands) - 1: 0},
        compiler_params=pltpu.CompilerParams(vmem_limit_bytes=32 * 1024 * 1024),
        cost_estimate=pl.CostEstimate(flops=cost, bytes_accessed=4 * 1024 * 1024, transcendentals=0),
    )(*operands)


def shards(tracers, emissions, winds, diffusivity, substeps, loader):
    tiles, groups = lax.axis_size("tile"), lax.axis_size("group")
    tile, group = lax.axis_index("tile"), lax.axis_index("group")
    even = tile % 2 == 0
    slot = loader[tile]
    scalars = jnp.stack(
        [
            substeps[jnp.maximum(tile - 1, 0)],
            substeps[tile],
            substeps[jnp.minimum(tile + 1, tiles - 1)],
            even.astype(jnp.int32),
            (tile == 0).astype(jnp.int32),
        ]
    )

    levels = winds.shape[2]
    half = levels // 2
    padded = jnp.pad(diffusivity, ((0, 0), (0, 1), (0, 0), (0, 0)))
    met = jnp.concatenate([winds[0], padded], axis=0)
    low, high = met[:, :half], met[:, half:]
    core = group % 2 == 1
    other = exchange(jnp.where(core, low, high), "group", 1)
    met = jnp.where(slot % 2 == group % 2, jnp.where(core, high, low), other)
    bit = 2
    while bit < groups:
        other = exchange(met, "group", bit)
        met = jnp.where((slot & bit) == (group & bit), met, other)
        bit *= 2
    wind_pair = exchange(met[:2], "tile", 1)
    wind_far = relay(wind_pair, "tile")
    bundle = jnp.concatenate([met, wind_pair, wind_far], axis=0)
    other = exchange(bundle, "group", 1)
    bundle = jnp.concatenate(
        [jnp.where(core, other, bundle), jnp.where(core, bundle, other)], axis=1
    )
    winds_here = (bundle[:2], bundle[3:5], bundle[5:7])
    mixing_coef = bundle[2]

    start = 0
    result = None
    for count, way in PARTS:
        part = tracers[start : start + count]
        if way == "relay":
            pair = exchange(part, "tile", 1)
            far = relay(pair, "tile")
        else:
            up, down = shift(part, "tile", 1), shift(part, "tile", -1)
            pair, far = jnp.where(even, down, up), jnp.where(even, up, down)
        result = window(
            scalars, tracers, emissions, start, count, pair, far, winds_here, mixing_coef, result
        )
        start += count
    return result


def solution(mesh):
    return jax.shard_map(
        shards,
        mesh=mesh,
        in_specs=(
            P("group", None, "tile", None),
            P("group", "tile", None),
            P("group", None, None, "tile", None),
            P("group", None, "tile", None),
            P(),
            P(),
        ),
        out_specs=P("group", None, "tile", None),
        check_vma=False,
    )
```

```python
import functools

import jax
import jax.numpy as jnp
from jax import lax
from jax.experimental import pallas as pl
from jax.experimental.pallas import tpu as pltpu
from jax.sharding import PartitionSpec as P

ROUNDS = 6
DEEP = 8
RELAYED = (3, 3)
STRAIGHT = 2
VMEM_LIMIT = 32 * 1024 * 1024


def exchange(value, axis, bit):
    count = lax.axis_size(axis)
    return lax.ppermute(value, axis, [(i, i ^ bit) for i in range(count)])


def shift(value, axis, by):
    count = lax.axis_size(axis)
    return lax.ppermute(value, axis, [(i, i + by) for i in range(count) if 0 <= i + by < count])


def relay(value, axis):
    count = lax.axis_size(axis)
    pairs = [(i, i + 2) for i in range(0, count - 2, 2)] + [(i, i - 2) for i in range(3, count, 2)]
    return lax.ppermute(value, axis, pairs)


def in_vmem(values):
    return [pltpu.with_memory_space_constraint(value, pltpu.VMEM) for value in values]


def counts_of(substeps, tile, tiles):
    south, north = jnp.maximum(tile - 1, 0), jnp.minimum(tile + 1, tiles - 1)
    return [substeps[south], substeps[tile], substeps[north]]


def first_choice_kernel(loader, wind, wind_other, diffusion, diffusion_other, *rest):
    out = rest[-1]
    slot, group = loader[lax.axis_index("tile")], lax.axis_index("group")
    mine = slot % 2 == group % 2
    half = out.shape[1]
    base = group % 2 * half
    for k in range(half):
        for kind in range(2):
            out[kind, k] = jnp.where(mine, wind[0, kind, base + k], wind_other[0, kind, base + k])
        at = jnp.minimum(base + k, diffusion.shape[1] - 1)
        out[2, k] = jnp.where(mine, diffusion[0, at], diffusion_other[0, at])


def next_choice_kernel(bit, loader, met, other, out):
    slot, group = loader[lax.axis_index("tile")], lax.axis_index("group")
    out[...] = jnp.where((slot & bit) == (group & bit), met[...], other[...])


def last_choice_kernel(bit, loader, met, other, *rest):
    wind, up, down, mix = rest[-4:]
    slot, group = loader[lax.axis_index("tile")], lax.axis_index("group")
    mine = (slot & bit) == (group & bit)
    _, height, deep, width = wind.shape
    reach = up.shape[1]
    for kind in range(2):
        for j in range(height):
            value = jnp.where(mine, met[kind, :, j, :], other[kind, :, j, :])
            wind[kind, j] = value
            if j < reach:
                down[kind, j] = value
            if j >= height - reach:
                up[kind, j - (height - reach)] = value
    mix[...] = jnp.where(mine, met[2], other[2])


def pack_kernel(relayed, tracers, *outs):
    even = lax.axis_index("tile") % 2 == 0
    _, levels, height, _ = tracers.shape
    rest, up, down = outs[-3:]
    reach = up.shape[2]
    skip = height - reach
    for g in range(levels // DEEP):
        deep = slice(g * DEEP, (g + 1) * DEEP)
        start = 0
        for part, count in zip(outs, relayed):
            for n in range(start, start + count):
                rows = [tracers[n, deep, j, :] for j in range(height)]
                for j in range(reach):
                    part[n - start, g, j] = jnp.where(even, rows[j], rows[j + skip])
                for j in range(skip):
                    rest[n, g, j] = jnp.where(even, rows[reach + j], rows[j])
            start += count
        for n in range(up.shape[0]):
            for j in range(reach):
                up[n, g, j] = tracers[start + n, deep, skip + j, :]
                down[n, g, j] = tracers[start + n, deep, j, :]


def on_core(kernel, scalars, operands, out_shape, waits=(), cost=1):
    vmem = pl.BlockSpec(memory_space=pltpu.VMEM)
    return pl.pallas_call(
        kernel,
        out_shape=out_shape,
        in_specs=[pl.BlockSpec(memory_space=pltpu.SMEM)] * len(scalars)
        + [vmem] * len(operands)
        + [pl.BlockSpec(memory_space=pl.ANY)] * len(waits),
        out_specs=jax.tree.map(lambda _: vmem, out_shape),
        compiler_params=pltpu.CompilerParams(vmem_limit_bytes=VMEM_LIMIT),
        cost_estimate=pl.CostEstimate(
            flops=0, bytes_accessed=cost * 1024 * 1024, transcendentals=0
        ),
    )(*scalars, *in_vmem(operands), *waits)


def prepare_kernel(tiles, substeps, own, own_other, up, up_other, down, down_other, mix, mix_other, *rest):
    coef, solve, faces, mixing = rest[-4:]
    _, height, _, width = own.shape
    reach = up.shape[1]
    groups = 2
    levels = groups * DEEP
    tile, core = lax.axis_index("tile"), lax.axis_index("group") % 2
    for g, here, south, north, mixed in (
        (core, own, up, down, mix),
        (1 - core, own_other, up_other, down_other, mix_other),
    ):
        for kind in range(2):
            for j in range(height):
                value = here[kind, j]
                if kind == 1 and j == 0:
                    value = jnp.where(tile == 0, 0.0, value)
                faces[kind, g, height + j] = value
            for j in range(reach):
                faces[kind, g, height - reach + j] = south[kind, j]
                faces[kind, g, 2 * height + j] = north[kind, j]
        for k in range(DEEP):
            mixing[g * DEEP + k] = mixed[k]
    counts = counts_of(substeps, tile, tiles)
    ones = jnp.ones((DEEP, width), jnp.float32)
    fractions = [ones / (ones * count.astype(jnp.float32)) for count in counts]
    reach -= 1
    for g in range(groups):
        for j in range(height - reach, 2 * height + reach):
            f = fractions[j // height]
            zonal, south, north = faces[0, g, j], faces[1, g, j], faces[1, g, j + 1]
            zonal_east = pltpu.roll(zonal, width - 1, 1)
            coef[g, j, 0] = 1.0 - f * (
                (jnp.maximum(zonal_east, 0.0) - jnp.minimum(zonal, 0.0))
                + (jnp.maximum(north, 0.0) - jnp.minimum(south, 0.0))
            )
            coef[g, j, 1] = f * jnp.maximum(zonal, 0.0)
            coef[g, j, 2] = -f * jnp.minimum(zonal_east, 0.0)
            coef[g, j, 3] = f * jnp.maximum(south, 0.0)
            coef[g, j, 4] = -f * jnp.minimum(north, 0.0)
    for j in range(height - reach, 2 * height + reach):
        coef[groups, j, 0] = ones
        for k in range(1, 5):
            coef[groups, j, k] = jnp.zeros_like(ones)
    ratio = lower = jnp.zeros((height, width), jnp.float32)
    for k in range(levels):
        upper = mixing[k] if k < levels - 1 else jnp.zeros_like(lower)
        pivot = 1.0 / (1.0 + lower + upper - lower * ratio)
        ratio = upper * pivot
        solve[k, 0] = lower
        solve[k, 1] = pivot
        solve[k, 2] = ratio
        lower = upper


def prepare(tiles, substeps, winds, mix, waits):
    _, height, half, width = winds[0].shape
    vmem = pl.BlockSpec(memory_space=pltpu.VMEM)
    return pl.pallas_call(
        functools.partial(prepare_kernel, tiles),
        out_shape=(
            pltpu.VMEM((3, 3 * height, 5, DEEP, width), jnp.float32),
            pltpu.VMEM((2 * half, 3, height, width), jnp.float32),
        ),
        in_specs=[pl.BlockSpec(memory_space=pltpu.SMEM)]
        + [vmem] * 8
        + [pl.BlockSpec(memory_space=pl.ANY)] * len(waits),
        out_specs=(vmem, vmem),
        scratch_shapes=[
            pltpu.VMEM((2, 2, 3 * height, DEEP, width), jnp.float32),
            pltpu.VMEM((2 * half, height, width), jnp.float32),
        ],
        compiler_params=pltpu.CompilerParams(vmem_limit_bytes=VMEM_LIMIT),
        cost_estimate=pl.CostEstimate(flops=0, bytes_accessed=4 * 1024 * 1024, transcendentals=0),
    )(substeps, *in_vmem([*winds, *mix]), *waits)


def window_kernel(start, last, tiles, substeps, coef, solve, own, source, *rest):
    if last:
        up, down, prior, out, field, advected, values, solved, sem = rest
        early = pltpu.make_async_copy(prior.at[:start], out.at[:start], sem.at[0])
        early.start()
        tracers, reach = up.shape[0], up.shape[2]
    else:
        pair, pair_rest, far, *rest = rest
        out, field, advected, values = rest[-4:]
        tracers, reach = pair.shape[0], pair.shape[2]
    _, levels, height, width = own.shape
    groups = levels // DEEP
    tile = lax.axis_index("tile")
    even = tile % 2 == 0
    pair_at = jnp.where(even, 3 * height - reach, 0)
    rest_at = jnp.where(even, 2 * height, reach)
    far_at = jnp.where(even, height - reach, 2 * height)
    counts = counts_of(substeps, tile, tiles)
    for n in range(tracers):
        for g in range(groups):
            deep = slice(g * DEEP, (g + 1) * DEEP)
            for j in range(height):
                field[0, n, g, height + j] = own[start + n, deep, j, :]
            for j in range(reach):
                if last:
                    field[0, n, g, height - reach + j] = up[n, g, j]
                    field[0, n, g, 2 * height + j] = down[n, g, j]
                else:
                    field[0, n, g, pair_at + j] = pair[n, g, j]
                    field[0, n, g, far_at + j] = far[n, g, j]
            if not last:
                for j in range(height - reach):
                    field[0, n, g, rest_at + j] = pair_rest[start + n, g, j]
    for step in range(ROUNDS):
        reach = ROUNDS - 1 - step
        low, high = height - reach, 2 * height + reach
        src, dst = step % 2, (step + 1) % 2
        for g in range(groups):
            pages = [jnp.where(step < count, g, groups) for count in counts]
            south = [field[src, n, g, low - 1] for n in range(tracers)]
            here = [field[src, n, g, low] for n in range(tracers)]
            for j in range(low, high):
                c = [coef[pages[j // height], j, k] for k in range(5)]
                for n in range(tracers):
                    north = field[src, n, g, j + 1]
                    new = (
                        c[0] * here[n]
                        + c[1] * pltpu.roll(here[n], 1, 1)
                        + c[2] * pltpu.roll(here[n], width - 1, 1)
                        + c[3] * south[n]
                        + c[4] * north
                    )
                    if step < ROUNDS - 1:
                        field[dst, n, g, j] = new
                    else:
                        advected[n, g * DEEP : (g + 1) * DEEP, j - height, :] = new
                    south[n], here[n] = here[n], north
    for k in range(levels):
        lower, pivot = solve[k, 0], solve[k, 1]
        for n in range(tracers):
            q = advected[n, k]
            q = q + (source[start + n] if k == 0 else lower * values[n, k - 1])
            values[n, k] = q * pivot
    for n in range(tracers):
        target = solved.at[n] if last else out.at[start + n]
        current = values[n, levels - 1]
        target[levels - 1] = current
        for k in range(levels - 2, -1, -1):
            current = values[n, k] + solve[k, 2] * current
            target[k] = current
    if last:
        late = pltpu.make_async_copy(solved, out.at[start:], sem.at[1])
        late.start()
        early.wait()
        late.wait()


def window(tiles, substeps, coef, solve, tracers, emissions, start, halos, prior):
    total, levels, height, width = tracers.shape
    count = halos[0].shape[0]
    groups = levels // DEEP
    last = start + count == total
    vmem = pl.BlockSpec(memory_space=pltpu.VMEM)
    operands = [coef, solve, tracers, emissions, *halos]
    scratch = [
        pltpu.VMEM((2, count, groups, 3 * height, DEEP, width), jnp.float32),
        pltpu.VMEM((count, levels, height, width), jnp.float32),
        pltpu.VMEM((count, levels, height, width), jnp.float32),
    ]
    aliases = {}
    if prior is not None:
        operands.append(prior)
        if not last:
            aliases = {len(operands): 0}
    if last:
        scratch += [
            pltpu.VMEM((count, levels, height, width), jnp.float32),
            pltpu.SemaphoreType.DMA((2,)),
        ]
    shape = tracers.shape
    return pl.pallas_call(
        functools.partial(window_kernel, start, last, tiles),
        out_shape=jax.ShapeDtypeStruct(shape, jnp.float32)
        if last
        else pltpu.VMEM(shape, jnp.float32),
        in_specs=[pl.BlockSpec(memory_space=pltpu.SMEM)] + [vmem] * len(operands),
        out_specs=pl.BlockSpec(memory_space=pl.ANY) if last else vmem,
        scratch_shapes=scratch,
        input_output_aliases=aliases,
        compiler_params=pltpu.CompilerParams(vmem_limit_bytes=VMEM_LIMIT),
        cost_estimate=pl.CostEstimate(
            flops=0, bytes_accessed=(2 + 4 * count) * 1024 * 1024, transcendentals=0
        ),
    )(substeps, *in_vmem(operands))


def shards(tracers, emissions, winds, diffusivity, substeps, loader):
    tiles, groups = lax.axis_size("tile"), lax.axis_size("group")
    _, levels, height, width = tracers.shape
    half = levels // 2
    relayed = sum(RELAYED)

    def rows_of(count, rows):
        return pltpu.VMEM((count, levels // DEEP, rows, DEEP, width), jnp.float32)

    *parts, rest, up, down = on_core(
        functools.partial(pack_kernel, RELAYED),
        [],
        [tracers],
        [rows_of(count, ROUNDS) for count in RELAYED]
        + [rows_of(relayed, height - ROUNDS), rows_of(STRAIGHT, ROUNDS), rows_of(STRAIGHT, ROUNDS)],
    )

    met = on_core(
        first_choice_kernel,
        [loader],
        [winds, exchange(winds, "group", 1), diffusivity, exchange(diffusivity, "group", 1)],
        pltpu.VMEM((3, half, height, width), jnp.float32),
    )
    bit = 2
    while 2 * bit < groups:
        met = on_core(
            functools.partial(next_choice_kernel, bit),
            [loader],
            [met, exchange(met, "group", bit)],
            pltpu.VMEM(met.shape, jnp.float32),
        )
        bit *= 2
    wind, wind_up, wind_down, mix = on_core(
        functools.partial(last_choice_kernel, bit),
        [loader],
        [met, exchange(met, "group", bit)],
        [
            pltpu.VMEM((2, height, half, width), jnp.float32),
            pltpu.VMEM((2, ROUNDS, half, width), jnp.float32),
            pltpu.VMEM((2, ROUNDS, half, width), jnp.float32),
            pltpu.VMEM((half, height, width), jnp.float32),
        ],
    )
    known = []
    for mine in (wind, shift(wind_up, "tile", 1), shift(wind_down, "tile", -1)):
        known += [mine, exchange(mine, "group", 1)]
    coef, solve = prepare(tiles, substeps, known, [mix, exchange(mix, "group", 1)], [])

    pairs = [exchange(part, "tile", 1) for part in parts]
    pair_rest = exchange(rest, "tile", 1)
    halos = [(pair, pair_rest, relay(pair, "tile")) for pair in pairs]
    halos.append((shift(up, "tile", 1), shift(down, "tile", -1)))
    result, start = None, 0
    for halo in halos:
        result = window(tiles, substeps, coef, solve, tracers, emissions, start, halo, result)
        start += halo[0].shape[0]
    return result


def solution(mesh):
    return jax.shard_map(
        shards,
        mesh=mesh,
        in_specs=(
            P("group", None, "tile", None),
            P("group", "tile", None),
            P("group", None, None, "tile", None),
            P("group", None, "tile", None),
            P(),
            P(),
        ),
        out_specs=P("group", None, "tile", None),
        check_vma=False,
    )
```

```python
import functools

import jax
import jax.numpy as jnp
from jax import lax
from jax.experimental import pallas as pl
from jax.experimental.pallas import tpu as pltpu
from jax.sharding import PartitionSpec as P

ROUNDS = 6
DEEP = 8
RELAYED = (4,)
WITH_WINDS = 1
STRAIGHT = 3
MIB = 1024 * 1024
VMEM_LIMIT = 32 * MIB
WINDOW_COST = 1
PREPARE_COST = 1


def exchange(value, axis, bit):
    count = lax.axis_size(axis)
    return lax.ppermute(value, axis, [(i, i ^ bit) for i in range(count)])


def shift(value, axis, by):
    count = lax.axis_size(axis)
    return lax.ppermute(value, axis, [(i, i + by) for i in range(count) if 0 <= i + by < count])


def relay(value, axis):
    count = lax.axis_size(axis)
    pairs = [(i, i + 2) for i in range(0, count - 2, 2)] + [(i, i - 2) for i in range(3, count, 2)]
    return lax.ppermute(value, axis, pairs)


def in_smem(value):
    return pltpu.with_memory_space_constraint(value, pltpu.SMEM)


def in_vmem(values):
    return [pltpu.with_memory_space_constraint(value, pltpu.VMEM) for value in values]


def first_choice_kernel(numbers, wind, wind_other, diffusion, diffusion_other, *rest):
    out = rest[-1]
    slot, group = numbers[0], lax.axis_index("group")
    mine = slot % 2 == group % 2
    half = out.shape[1]
    base = group % 2 * half
    for k in range(half):
        for kind in range(2):
            out[kind, k] = jnp.where(mine, wind[0, kind, base + k], wind_other[0, kind, base + k])
        at = jnp.minimum(base + k, diffusion.shape[1] - 1)
        out[2, k] = jnp.where(mine, diffusion[0, at], diffusion_other[0, at])


def next_choice_kernel(bit, numbers, met, other, out):
    slot, group = numbers[0], lax.axis_index("group")
    out[...] = jnp.where((slot & bit) == (group & bit), met[...], other[...])


def last_choice_kernel(bit, numbers, met, other, tracers_up, tracers_down, *rest):
    wind, up, down, mix = rest[-4:]
    group = lax.axis_index("group")
    mine = (numbers[0] & bit) == (group & bit)
    _, height, deep, width = wind.shape
    count, groups, reach = tracers_up.shape[:3]
    for kind in range(2):
        for j in range(height):
            value = jnp.where(mine, met[kind, :, j, :], other[kind, :, j, :])
            wind[kind, j] = value
            if j < reach:
                down[kind * reach + j] = value
            if j >= height - reach:
                up[kind * reach + j - (height - reach)] = value
    mix[...] = jnp.where(mine, met[2], other[2])
    for n in range(count):
        for g in range(groups):
            at = (2 + n * groups + g) * reach
            up[at : at + reach] = tracers_up[n, g]
            down[at : at + reach] = tracers_down[n, g]


def onward_kernel(_, pair, *rest):
    out = rest[-1]
    tracers, groups, reach = out.shape[:3]
    skip = jnp.where(lax.axis_index("tile") % 2 == 0, pair.shape[2] - reach, 0)
    for n in range(tracers):
        for g in range(groups):
            out[n, g] = pair[n, g, pl.ds(skip, reach)]


def pack_kernel(relayed, tiles, substeps_in, loader_in, tracers_in, wind_in, diffusion_in, *rest):
    numbers, tracers, wind, diffusion, *outs, substeps, loader, sem = rest
    copies = [
        pltpu.make_async_copy(source, target, sem.at[i])
        for i, (source, target) in enumerate(
            (
                (substeps_in, substeps),
                (loader_in, loader),
                (tracers_in, tracers),
                (wind_in, wind),
                (diffusion_in, diffusion),
            )
        )
    ]
    for copy in copies:
        copy.start()
    tile = lax.axis_index("tile")
    _, levels, height, _ = tracers.shape
    straight = [outs[-4:-2], outs[-2:]]
    reach = outs[-1].shape[2]
    copies[2].wait()
    for g in range(levels // DEEP):
        deep = slice(g * DEEP, (g + 1) * DEEP)
        start = 0
        for part, count in zip(outs, relayed):
            for n in range(count):
                for j in range(height):
                    part[n, g, j] = tracers[start + n, deep, j, :]
            start += count
        for up, down in straight:
            for n in range(up.shape[0]):
                for j in range(reach):
                    up[n, g, j] = tracers[start + n, deep, height - reach + j, :]
                    down[n, g, j] = tracers[start + n, deep, j, :]
            start += up.shape[0]
    copies[0].wait()
    copies[1].wait()
    numbers[0] = loader[tile]
    numbers[1] = substeps[jnp.maximum(tile - 1, 0)]
    numbers[2] = substeps[tile]
    numbers[3] = substeps[jnp.minimum(tile + 1, tiles - 1)]
    copies[3].wait()
    copies[4].wait()


def pack(tiles, substeps, loader, tracers, winds, diffusivity):
    _, levels, height, width = tracers.shape

    def rows_of(count, rows):
        return pltpu.VMEM((count, levels // DEEP, rows, DEEP, width), jnp.float32)

    out_shape = [pltpu.SMEM((4,), jnp.int32)]
    out_shape += [pltpu.VMEM(x.shape, x.dtype) for x in (tracers, winds, diffusivity)]
    out_shape += [rows_of(count, height) for count in RELAYED]
    out_shape += [rows_of(WITH_WINDS, ROUNDS)] * 2 + [rows_of(STRAIGHT, ROUNDS)] * 2
    vmem = pl.BlockSpec(memory_space=pltpu.VMEM)
    smem = pl.BlockSpec(memory_space=pltpu.SMEM)
    hbm = pl.BlockSpec(memory_space=pltpu.HBM)
    return pl.pallas_call(
        functools.partial(pack_kernel, RELAYED, tiles),
        out_shape=out_shape,
        in_specs=[hbm] * 5,
        out_specs=[smem] + [vmem] * (len(out_shape) - 1),
        scratch_shapes=[
            pltpu.SMEM(substeps.shape, jnp.int32),
            pltpu.SMEM(loader.shape, jnp.int32),
            pltpu.SemaphoreType.DMA((5,)),
        ],
        compiler_params=pltpu.CompilerParams(vmem_limit_bytes=VMEM_LIMIT),
        cost_estimate=pl.CostEstimate(flops=0, bytes_accessed=MIB, transcendentals=0),
    )(
        *[
            pltpu.with_memory_space_constraint(x, pltpu.HBM)
            for x in (substeps, loader, tracers, winds, diffusivity)
        ]
    )


def on_core(kernel, numbers, operands, out_shape, waits=(), cost=1):
    vmem = pl.BlockSpec(memory_space=pltpu.VMEM)
    return pl.pallas_call(
        kernel,
        out_shape=out_shape,
        in_specs=[pl.BlockSpec(memory_space=pltpu.SMEM)]
        + [vmem] * len(operands)
        + [pl.BlockSpec(memory_space=pl.ANY)] * len(waits),
        out_specs=jax.tree.map(lambda _: vmem, out_shape),
        compiler_params=pltpu.CompilerParams(vmem_limit_bytes=VMEM_LIMIT),
        cost_estimate=pl.CostEstimate(
            flops=0, bytes_accessed=cost * MIB, transcendentals=0
        ),
    )(in_smem(numbers), *in_vmem(operands), *waits)


def gather_kernel(_, wind, up, down, mix, *rest):
    height = wind.shape[1]
    half = height // 2
    rows = rest[-1].shape[0] - half
    reach = (rows - height) // 2
    for kind, out in enumerate(rest[-2:]):
        out[:reach] = up[pl.ds(kind * reach, reach)]
        out[pl.ds(reach, height)] = wind[kind]
        out[pl.ds(reach + height, reach)] = down[pl.ds(kind * reach, reach)]
        out[rows:] = mix[pl.ds(kind * half, half)]


def prepare_kernel(height, reach, numbers, *rest):
    *blocks, coef, solve, faces, mixing = rest
    width = coef.shape[-1]
    groups = 2
    levels = groups * DEEP
    rows = height + 2 * reach
    half = height // 2
    tile, core = lax.axis_index("tile"), lax.axis_index("group") % 2
    for g, pair in ((core, blocks[:2]), (1 - core, blocks[2:4])):
        for kind, block in enumerate(pair):
            for j in range(rows):
                value = block[j]
                if kind == 1 and j == reach:
                    value = jnp.where(tile == 0, 0.0, value)
                faces[kind, g, height - reach + j] = value
            for k in range(half):
                mixing[g * DEEP + kind * half + k] = block[rows + k]
    counts = [numbers[t] for t in range(1, 4)]
    ones = jnp.ones((DEEP, width), jnp.float32)
    fractions = [ones / (ones * count.astype(jnp.float32)) for count in counts]
    reach -= 1
    for g in range(groups):
        for j in range(height - reach, 2 * height + reach):
            f = fractions[j // height]
            zonal, south, north = faces[0, g, j], faces[1, g, j], faces[1, g, j + 1]
            zonal_east = pltpu.roll(zonal, width - 1, 1)
            coef[g, j, 0] = 1.0 - f * (
                (jnp.maximum(zonal_east, 0.0) - jnp.minimum(zonal, 0.0))
                + (jnp.maximum(north, 0.0) - jnp.minimum(south, 0.0))
            )
            coef[g, j, 1] = f * jnp.maximum(zonal, 0.0)
            coef[g, j, 2] = -f * jnp.minimum(zonal_east, 0.0)
            coef[g, j, 3] = f * jnp.maximum(south, 0.0)
            coef[g, j, 4] = -f * jnp.minimum(north, 0.0)
    for j in range(height - reach, 2 * height + reach):
        coef[groups, j, 0] = ones
        for k in range(1, 5):
            coef[groups, j, k] = jnp.zeros_like(ones)
    ratio = lower = jnp.zeros((height, width), jnp.float32)
    for k in range(levels):
        upper = mixing[k] if k < levels - 1 else jnp.zeros_like(lower)
        pivot = 1.0 / (1.0 + lower + upper - lower * ratio)
        ratio = upper * pivot
        solve[k, 0] = lower
        solve[k, 1] = pivot
        solve[k, 2] = ratio
        lower = upper


def prepare(numbers, height, reach, blocks, waits):
    width = blocks[0].shape[-1]
    vmem = pl.BlockSpec(memory_space=pltpu.VMEM)
    return pl.pallas_call(
        functools.partial(prepare_kernel, height, reach),
        out_shape=(
            pltpu.VMEM((3, 3 * height, 5, DEEP, width), jnp.float32),
            pltpu.VMEM((2 * DEEP, 3, height, width), jnp.float32),
        ),
        in_specs=[pl.BlockSpec(memory_space=pltpu.SMEM)]
        + [vmem] * len(blocks)
        + [pl.BlockSpec(memory_space=pl.ANY)] * len(waits),
        out_specs=(vmem, vmem),
        scratch_shapes=[
            pltpu.VMEM((2, 2, 3 * height, DEEP, width), jnp.float32),
            pltpu.VMEM((2 * DEEP, height, width), jnp.float32),
        ],
        compiler_params=pltpu.CompilerParams(vmem_limit_bytes=VMEM_LIMIT),
        cost_estimate=pl.CostEstimate(
            flops=0, bytes_accessed=PREPARE_COST * MIB, transcendentals=0
        ),
    )(in_smem(numbers), *in_vmem(blocks), *waits)


def window_kernel(way, start, count, last, numbers, coef, solve, own, source, *rest):
    first, second, *rest = rest
    if last:
        prior, out, field, advected, values, solved, sem = rest
        early = pltpu.make_async_copy(prior.at[:start], out.at[:start], sem.at[0])
        early.start()
    else:
        out, field, advected, values = rest[-4:]
    tracers = count
    reach = ROUNDS
    _, levels, height, width = own.shape
    groups = levels // DEEP
    tile = lax.axis_index("tile")
    even = tile % 2 == 0
    pair_at = jnp.where(even, 2 * height, 0)
    far_at = jnp.where(even, height - reach, 2 * height)
    counts = [numbers[t] for t in range(1, 4)]
    for n in range(tracers):
        for g in range(groups):
            deep = slice(g * DEEP, (g + 1) * DEEP)
            for j in range(height):
                field[0, n, g, height + j] = own[start + n, deep, j, :]
            for j in range(reach):
                if way == "relay":
                    field[0, n, g, far_at + j] = second[n, g, j]
                else:
                    if way == "winds":
                        at = (2 + n * groups + g) * reach + j
                        south, north = first[at], second[at]
                    else:
                        south, north = first[n, g, j], second[n, g, j]
                    field[0, n, g, height - reach + j] = south
                    field[0, n, g, 2 * height + j] = north
            if way == "relay":
                for j in range(height):
                    field[0, n, g, pair_at + j] = first[n, g, j]
    for step in range(ROUNDS):
        reach = ROUNDS - 1 - step
        low, high = height - reach, 2 * height + reach
        src, dst = step % 2, (step + 1) % 2
        for g in range(groups):
            pages = [jnp.where(step < count, g, groups) for count in counts]
            south = [field[src, n, g, low - 1] for n in range(tracers)]
            here = [field[src, n, g, low] for n in range(tracers)]
            for j in range(low, high):
                c = [coef[pages[j // height], j, k] for k in range(5)]
                for n in range(tracers):
                    north = field[src, n, g, j + 1]
                    new = (
                        c[0] * here[n]
                        + c[1] * pltpu.roll(here[n], 1, 1)
                        + c[2] * pltpu.roll(here[n], width - 1, 1)
                        + c[3] * south[n]
                        + c[4] * north
                    )
                    if step < ROUNDS - 1:
                        field[dst, n, g, j] = new
                    else:
                        advected[n, g * DEEP : (g + 1) * DEEP, j - height, :] = new
                    south[n], here[n] = here[n], north
    for k in range(levels):
        lower, pivot = solve[k, 0], solve[k, 1]
        for n in range(tracers):
            q = advected[n, k]
            q = q + (source[start + n] if k == 0 else lower * values[n, k - 1])
            values[n, k] = q * pivot
    for n in range(tracers):
        target = solved.at[n] if last else out.at[start + n]
        current = values[n, levels - 1]
        target[levels - 1] = current
        for k in range(levels - 2, -1, -1):
            current = values[n, k] + solve[k, 2] * current
            target[k] = current
    if last:
        late = pltpu.make_async_copy(solved, out.at[start:], sem.at[1])
        late.start()
        early.wait()
        late.wait()


def window(numbers, coef, solve, tracers, emissions, way, start, count, halos, prior):
    total, levels, height, width = tracers.shape
    groups = levels // DEEP
    last = start + count == total
    vmem = pl.BlockSpec(memory_space=pltpu.VMEM)
    operands = [coef, solve, tracers, emissions, *halos]
    scratch = [
        pltpu.VMEM((2, count, groups, 3 * height, DEEP, width), jnp.float32),
        pltpu.VMEM((count, levels, height, width), jnp.float32),
        pltpu.VMEM((count, levels, height, width), jnp.float32),
    ]
    aliases = {}
    if prior is not None:
        operands.append(prior)
        if not last:
            aliases = {len(operands): 0}
    if last:
        scratch += [
            pltpu.VMEM((count, levels, height, width), jnp.float32),
            pltpu.SemaphoreType.DMA((2,)),
        ]
    shape = tracers.shape
    return pl.pallas_call(
        functools.partial(window_kernel, way, start, count, last),
        out_shape=jax.ShapeDtypeStruct(shape, jnp.float32)
        if last
        else pltpu.VMEM(shape, jnp.float32),
        in_specs=[pl.BlockSpec(memory_space=pltpu.SMEM)] + [vmem] * len(operands),
        out_specs=pl.BlockSpec(memory_space=pl.ANY) if last else vmem,
        scratch_shapes=scratch,
        input_output_aliases=aliases,
        compiler_params=pltpu.CompilerParams(vmem_limit_bytes=VMEM_LIMIT),
        cost_estimate=pl.CostEstimate(
            flops=0, bytes_accessed=WINDOW_COST * MIB, transcendentals=0
        ),
    )(in_smem(numbers), *in_vmem(operands))


def shards(tracers, emissions, winds, diffusivity, substeps, loader):
    tiles, groups = lax.axis_size("tile"), lax.axis_size("group")
    _, levels, height, width = tracers.shape
    half = levels // 2
    wind_other, diffusion_other = exchange(winds, "group", 1), exchange(diffusivity, "group", 1)
    numbers, tracers, winds, diffusivity, *parts, up_first, down_first, up, down = pack(
        tiles, substeps, loader, tracers, winds, diffusivity
    )

    pairs = [exchange(part, "tile", 1) for part in parts]
    halos = []
    for pair in pairs:
        shape = (pair.shape[0], pair.shape[1], ROUNDS, *pair.shape[3:])
        onward = on_core(onward_kernel, numbers, [pair], pltpu.VMEM(shape, jnp.float32))
        halos.append(("relay", pair.shape[0], (pair, relay(onward, "tile"))))

    met = on_core(
        first_choice_kernel,
        numbers,
        [winds, wind_other, diffusivity, diffusion_other],
        pltpu.VMEM((3, half, height, width), jnp.float32),
    )
    bit = 2
    while 2 * bit < groups:
        met = on_core(
            functools.partial(next_choice_kernel, bit),
            numbers,
            [met, exchange(met, "group", bit)],
            pltpu.VMEM(met.shape, jnp.float32),
        )
        bit *= 2
    with_winds = 2 * ROUNDS * (1 + WITH_WINDS)
    wind, wind_up, wind_down, mix = on_core(
        functools.partial(last_choice_kernel, bit),
        numbers,
        [met, exchange(met, "group", bit), up_first, down_first],
        [
            pltpu.VMEM((2, height, half, width), jnp.float32),
            pltpu.VMEM((with_winds, half, width), jnp.float32),
            pltpu.VMEM((with_winds, half, width), jnp.float32),
            pltpu.VMEM((half, height, width), jnp.float32),
        ],
    )
    wind_up, wind_down = shift(wind_up, "tile", 1), shift(wind_down, "tile", -1)
    halos.append(("winds", WITH_WINDS, (wind_up, wind_down)))
    halos.append(("straight", STRAIGHT, (shift(up, "tile", 1), shift(down, "tile", -1))))
    known = on_core(
        gather_kernel,
        numbers,
        [wind, wind_up, wind_down, mix],
        [pltpu.VMEM((height + 2 * ROUNDS + height // 2, half, width), jnp.float32)] * 2,
    )
    coef, solve = prepare(
        numbers, height, ROUNDS, [*known, *(exchange(x, "group", 1) for x in known)], []
    )

    result, start = None, 0
    for way, count, halo in halos:
        result = window(
            numbers, coef, solve, tracers, emissions, way, start, count, halo, result
        )
        start += count
    return result


def solution(mesh):
    return jax.shard_map(
        shards,
        mesh=mesh,
        in_specs=(
            P("group", None, "tile", None),
            P("group", "tile", None),
            P("group", None, None, "tile", None),
            P("group", None, "tile", None),
            P(),
            P(),
        ),
        out_specs=P("group", None, "tile", None),
        check_vma=False,
    )
```

```python
import functools

import jax
import jax.numpy as jnp
from jax import lax
from jax.experimental import pallas as pl
from jax.experimental.pallas import tpu as pltpu
from jax.sharding import PartitionSpec as P

ROUNDS = 6
DEEP = 8
RELAYED = (4,)
WITH_WINDS = 1
STRAIGHT = 3
MIB = 1024 * 1024
VMEM_LIMIT = 32 * MIB
WINDOW_COST = 1
PREPARE_COST = 1


def exchange(value, axis, bit):
    count = lax.axis_size(axis)
    return lax.ppermute(value, axis, [(i, i ^ bit) for i in range(count)])


def cross(value, axis):
    count = lax.axis_size(axis)
    pairs = [(i, i + 1) for i in range(1, count - 1, 2)]
    return lax.ppermute(value, axis, pairs + [(j, i) for i, j in pairs])


def relay(value, axis):
    count = lax.axis_size(axis)
    pairs = [(i, i + 2) for i in range(0, count - 2, 2)] + [(i, i - 2) for i in range(3, count, 2)]
    return lax.ppermute(value, axis, pairs)


def in_smem(value):
    return pltpu.with_memory_space_constraint(value, pltpu.SMEM)


def in_vmem(values):
    return [pltpu.with_memory_space_constraint(value, pltpu.VMEM) for value in values]


def first_choice_kernel(numbers, wind, wind_other, diffusion, diffusion_other, *rest):
    out = rest[-1]
    slot, group = numbers[0], lax.axis_index("group")
    mine = slot % 2 == group % 2
    half = out.shape[1]
    base = group % 2 * half
    for k in range(half):
        for kind in range(2):
            out[kind, k] = jnp.where(mine, wind[0, kind, base + k], wind_other[0, kind, base + k])
        at = jnp.minimum(base + k, diffusion.shape[1] - 1)
        out[2, k] = jnp.where(mine, diffusion[0, at], diffusion_other[0, at])


def next_choice_kernel(bit, numbers, met, other, out):
    slot, group = numbers[0], lax.axis_index("group")
    out[...] = jnp.where((slot & bit) == (group & bit), met[...], other[...])


def last_choice_kernel(bit, numbers, met, other, tracers_pair, tracers_far, *rest):
    wind, to_pair, to_far, mix = rest[-4:]
    group = lax.axis_index("group")
    mine = (numbers[0] & bit) == (group & bit)
    even = lax.axis_index("tile") % 2 == 0
    _, height, deep, width = wind.shape
    count, groups, reach = tracers_pair.shape[:3]
    for kind in range(2):
        rows = [
            jnp.where(mine, met[kind, :, j, :], other[kind, :, j, :]) for j in range(height)
        ]
        for j in range(height):
            wind[kind, j] = rows[j]
        for j in range(reach):
            last, first = rows[height - reach + j], rows[j]
            to_pair[kind * reach + j] = jnp.where(even, last, first)
            to_far[kind * reach + j] = jnp.where(even, first, last)
    mix[...] = jnp.where(mine, met[2], other[2])
    for n in range(count):
        for g in range(groups):
            at = (2 + n * groups + g) * reach
            to_pair[at : at + reach] = tracers_pair[n, g]
            to_far[at : at + reach] = tracers_far[n, g]


def onward_kernel(_, pair, *rest):
    out = rest[-1]
    tracers, groups, reach = out.shape[:3]
    skip = jnp.where(lax.axis_index("tile") % 2 == 0, pair.shape[2] - reach, 0)
    for n in range(tracers):
        for g in range(groups):
            out[n, g] = pair[n, g, pl.ds(skip, reach)]


def pack_kernel(relayed, tiles, substeps_in, loader_in, tracers_in, wind_in, diffusion_in, *rest):
    numbers, tracers, wind, diffusion, *outs, substeps, loader, sem = rest
    copies = [
        pltpu.make_async_copy(source, target, sem.at[i])
        for i, (source, target) in enumerate(
            (
                (substeps_in, substeps),
                (loader_in, loader),
                (tracers_in, tracers),
                (wind_in, wind),
                (diffusion_in, diffusion),
            )
        )
    ]
    for copy in copies:
        copy.start()
    tile = lax.axis_index("tile")
    even = tile % 2 == 0
    _, levels, height, _ = tracers.shape
    straight = [outs[-4:-2], outs[-2:]]
    reach = outs[-1].shape[2]
    copies[2].wait()
    for g in range(levels // DEEP):
        deep = slice(g * DEEP, (g + 1) * DEEP)
        start = 0
        for part, count in zip(outs, relayed):
            for n in range(count):
                for j in range(height):
                    part[n, g, j] = tracers[start + n, deep, j, :]
            start += count
        for to_pair, to_far in straight:
            for n in range(to_pair.shape[0]):
                rows = [tracers[start + n, deep, j, :] for j in range(height)]
                for j in range(reach):
                    last, first = rows[height - reach + j], rows[j]
                    to_pair[n, g, j] = jnp.where(even, last, first)
                    to_far[n, g, j] = jnp.where(even, first, last)
            start += to_pair.shape[0]
    copies[0].wait()
    copies[1].wait()
    numbers[0] = loader[tile]
    numbers[1] = substeps[jnp.maximum(tile - 1, 0)]
    numbers[2] = substeps[tile]
    numbers[3] = substeps[jnp.minimum(tile + 1, tiles - 1)]
    copies[3].wait()
    copies[4].wait()


def pack(tiles, substeps, loader, tracers, winds, diffusivity):
    _, levels, height, width = tracers.shape

    def rows_of(count, rows):
        return pltpu.VMEM((count, levels // DEEP, rows, DEEP, width), jnp.float32)

    out_shape = [pltpu.SMEM((4,), jnp.int32)]
    out_shape += [pltpu.VMEM(x.shape, x.dtype) for x in (tracers, winds, diffusivity)]
    out_shape += [rows_of(count, height) for count in RELAYED]
    out_shape += [rows_of(WITH_WINDS, ROUNDS)] * 2 + [rows_of(STRAIGHT, ROUNDS)] * 2
    vmem = pl.BlockSpec(memory_space=pltpu.VMEM)
    smem = pl.BlockSpec(memory_space=pltpu.SMEM)
    hbm = pl.BlockSpec(memory_space=pltpu.HBM)
    return pl.pallas_call(
        functools.partial(pack_kernel, RELAYED, tiles),
        out_shape=out_shape,
        in_specs=[hbm] * 5,
        out_specs=[smem] + [vmem] * (len(out_shape) - 1),
        scratch_shapes=[
            pltpu.SMEM(substeps.shape, jnp.int32),
            pltpu.SMEM(loader.shape, jnp.int32),
            pltpu.SemaphoreType.DMA((5,)),
        ],
        compiler_params=pltpu.CompilerParams(vmem_limit_bytes=VMEM_LIMIT),
        cost_estimate=pl.CostEstimate(flops=0, bytes_accessed=MIB, transcendentals=0),
    )(
        *[
            pltpu.with_memory_space_constraint(x, pltpu.HBM)
            for x in (substeps, loader, tracers, winds, diffusivity)
        ]
    )


def on_core(kernel, numbers, operands, out_shape, waits=(), cost=1):
    vmem = pl.BlockSpec(memory_space=pltpu.VMEM)
    return pl.pallas_call(
        kernel,
        out_shape=out_shape,
        in_specs=[pl.BlockSpec(memory_space=pltpu.SMEM)]
        + [vmem] * len(operands)
        + [pl.BlockSpec(memory_space=pl.ANY)] * len(waits),
        out_specs=jax.tree.map(lambda _: vmem, out_shape),
        compiler_params=pltpu.CompilerParams(vmem_limit_bytes=VMEM_LIMIT),
        cost_estimate=pl.CostEstimate(
            flops=0, bytes_accessed=cost * MIB, transcendentals=0
        ),
    )(in_smem(numbers), *in_vmem(operands), *waits)


def gather_kernel(_, wind, pair, far, mix, *rest):
    height = wind.shape[1]
    half = height // 2
    rows = rest[-1].shape[0] - half
    reach = (rows - height) // 2
    even = lax.axis_index("tile") % 2 == 0
    pair_at = jnp.where(even, reach + height, 0)
    far_at = jnp.where(even, 0, reach + height)
    for kind, out in enumerate(rest[-2:]):
        out[pl.ds(pair_at, reach)] = pair[pl.ds(kind * reach, reach)]
        out[pl.ds(reach, height)] = wind[kind]
        out[pl.ds(far_at, reach)] = far[pl.ds(kind * reach, reach)]
        out[rows:] = mix[pl.ds(kind * half, half)]


def prepare_kernel(height, reach, numbers, *rest):
    *blocks, coef, solve, faces, mixing = rest
    width = coef.shape[-1]
    groups = 2
    levels = groups * DEEP
    rows = height + 2 * reach
    half = height // 2
    tile, core = lax.axis_index("tile"), lax.axis_index("group") % 2
    for g, pair in ((core, blocks[:2]), (1 - core, blocks[2:4])):
        for kind, block in enumerate(pair):
            for j in range(rows):
                value = block[j]
                if kind == 1 and j == reach:
                    value = jnp.where(tile == 0, 0.0, value)
                faces[kind, g, height - reach + j] = value
            for k in range(half):
                mixing[g * DEEP + kind * half + k] = block[rows + k]
    counts = [numbers[t] for t in range(1, 4)]
    ones = jnp.ones((DEEP, width), jnp.float32)
    fractions = [ones / (ones * count.astype(jnp.float32)) for count in counts]
    reach -= 1
    for g in range(groups):
        for j in range(height - reach, 2 * height + reach):
            f = fractions[j // height]
            zonal, south, north = faces[0, g, j], faces[1, g, j], faces[1, g, j + 1]
            zonal_east = pltpu.roll(zonal, width - 1, 1)
            coef[g, j, 0] = 1.0 - f * (
                (jnp.maximum(zonal_east, 0.0) - jnp.minimum(zonal, 0.0))
                + (jnp.maximum(north, 0.0) - jnp.minimum(south, 0.0))
            )
            coef[g, j, 1] = f * jnp.maximum(zonal, 0.0)
            coef[g, j, 2] = -f * jnp.minimum(zonal_east, 0.0)
            coef[g, j, 3] = f * jnp.maximum(south, 0.0)
            coef[g, j, 4] = -f * jnp.minimum(north, 0.0)
    for j in range(height - reach, 2 * height + reach):
        coef[groups, j, 0] = ones
        for k in range(1, 5):
            coef[groups, j, k] = jnp.zeros_like(ones)
    ratio = lower = jnp.zeros((height, width), jnp.float32)
    for k in range(levels):
        upper = mixing[k] if k < levels - 1 else jnp.zeros_like(lower)
        pivot = 1.0 / (1.0 + lower + upper - lower * ratio)
        ratio = upper * pivot
        solve[k, 0] = lower
        solve[k, 1] = pivot
        solve[k, 2] = ratio
        lower = upper


def prepare(numbers, height, reach, blocks, waits):
    width = blocks[0].shape[-1]
    vmem = pl.BlockSpec(memory_space=pltpu.VMEM)
    return pl.pallas_call(
        functools.partial(prepare_kernel, height, reach),
        out_shape=(
            pltpu.VMEM((3, 3 * height, 5, DEEP, width), jnp.float32),
            pltpu.VMEM((2 * DEEP, 3, height, width), jnp.float32),
        ),
        in_specs=[pl.BlockSpec(memory_space=pltpu.SMEM)]
        + [vmem] * len(blocks)
        + [pl.BlockSpec(memory_space=pl.ANY)] * len(waits),
        out_specs=(vmem, vmem),
        scratch_shapes=[
            pltpu.VMEM((2, 2, 3 * height, DEEP, width), jnp.float32),
            pltpu.VMEM((2 * DEEP, height, width), jnp.float32),
        ],
        compiler_params=pltpu.CompilerParams(vmem_limit_bytes=VMEM_LIMIT),
        cost_estimate=pl.CostEstimate(
            flops=0, bytes_accessed=PREPARE_COST * MIB, transcendentals=0
        ),
    )(in_smem(numbers), *in_vmem(blocks), *waits)


def window_kernel(way, start, count, last, numbers, coef, solve, own, source, *rest):
    pair, far, *rest = rest
    if last:
        prior, out, field, advected, values, solved, sem = rest
        early = pltpu.make_async_copy(prior.at[:start], out.at[:start], sem.at[0])
        early.start()
    else:
        out, field, advected, values = rest[-4:]
    tracers = count
    reach = ROUNDS
    _, levels, height, width = own.shape
    groups = levels // DEEP
    tile = lax.axis_index("tile")
    even = tile % 2 == 0
    pair_at = jnp.where(even, 2 * height, 0 if way == "relay" else height - reach)
    far_at = jnp.where(even, height - reach, 2 * height)
    counts = [numbers[t] for t in range(1, 4)]
    for n in range(tracers):
        for g in range(groups):
            deep = slice(g * DEEP, (g + 1) * DEEP)
            for j in range(height):
                field[0, n, g, height + j] = own[start + n, deep, j, :]
            for j in range(reach):
                if way == "winds":
                    at = (2 + n * groups + g) * reach + j
                    near, distant = pair[at], far[at]
                else:
                    near, distant = pair[n, g, j], far[n, g, j]
                field[0, n, g, pair_at + j] = near
                field[0, n, g, far_at + j] = distant
            if way == "relay":
                for j in range(reach, height):
                    field[0, n, g, pair_at + j] = pair[n, g, j]
    for step in range(ROUNDS):
        reach = ROUNDS - 1 - step
        low, high = height - reach, 2 * height + reach
        src, dst = step % 2, (step + 1) % 2
        for g in range(groups):
            pages = [jnp.where(step < count, g, groups) for count in counts]
            south = [field[src, n, g, low - 1] for n in range(tracers)]
            here = [field[src, n, g, low] for n in range(tracers)]
            for j in range(low, high):
                c = [coef[pages[j // height], j, k] for k in range(5)]
                for n in range(tracers):
                    north = field[src, n, g, j + 1]
                    new = (
                        c[0] * here[n]
                        + c[1] * pltpu.roll(here[n], 1, 1)
                        + c[2] * pltpu.roll(here[n], width - 1, 1)
                        + c[3] * south[n]
                        + c[4] * north
                    )
                    if step < ROUNDS - 1:
                        field[dst, n, g, j] = new
                    else:
                        advected[n, g * DEEP : (g + 1) * DEEP, j - height, :] = new
                    south[n], here[n] = here[n], north
    for k in range(levels):
        lower, pivot = solve[k, 0], solve[k, 1]
        for n in range(tracers):
            q = advected[n, k]
            q = q + (source[start + n] if k == 0 else lower * values[n, k - 1])
            values[n, k] = q * pivot
    for n in range(tracers):
        target = solved.at[n] if last else out.at[start + n]
        current = values[n, levels - 1]
        target[levels - 1] = current
        for k in range(levels - 2, -1, -1):
            current = values[n, k] + solve[k, 2] * current
            target[k] = current
    if last:
        late = pltpu.make_async_copy(solved, out.at[start:], sem.at[1])
        late.start()
        early.wait()
        late.wait()


def window(numbers, coef, solve, tracers, emissions, way, start, count, halos, prior):
    total, levels, height, width = tracers.shape
    groups = levels // DEEP
    last = start + count == total
    vmem = pl.BlockSpec(memory_space=pltpu.VMEM)
    operands = [coef, solve, tracers, emissions, *halos]
    scratch = [
        pltpu.VMEM((2, count, groups, 3 * height, DEEP, width), jnp.float32),
        pltpu.VMEM((count, levels, height, width), jnp.float32),
        pltpu.VMEM((count, levels, height, width), jnp.float32),
    ]
    aliases = {}
    if prior is not None:
        operands.append(prior)
        if not last:
            aliases = {len(operands): 0}
    if last:
        scratch += [
            pltpu.VMEM((count, levels, height, width), jnp.float32),
            pltpu.SemaphoreType.DMA((2,)),
        ]
    shape = tracers.shape
    return pl.pallas_call(
        functools.partial(window_kernel, way, start, count, last),
        out_shape=jax.ShapeDtypeStruct(shape, jnp.float32)
        if last
        else pltpu.VMEM(shape, jnp.float32),
        in_specs=[pl.BlockSpec(memory_space=pltpu.SMEM)] + [vmem] * len(operands),
        out_specs=pl.BlockSpec(memory_space=pl.ANY) if last else vmem,
        scratch_shapes=scratch,
        input_output_aliases=aliases,
        compiler_params=pltpu.CompilerParams(vmem_limit_bytes=VMEM_LIMIT),
        cost_estimate=pl.CostEstimate(
            flops=0, bytes_accessed=WINDOW_COST * MIB, transcendentals=0
        ),
    )(in_smem(numbers), *in_vmem(operands))


def shards(tracers, emissions, winds, diffusivity, substeps, loader):
    tiles, groups = lax.axis_size("tile"), lax.axis_size("group")
    _, levels, height, width = tracers.shape
    half = levels // 2
    wind_other, diffusion_other = exchange(winds, "group", 1), exchange(diffusivity, "group", 1)
    numbers, tracers, winds, diffusivity, *parts, pair_first, far_first, to_pair, to_far = pack(
        tiles, substeps, loader, tracers, winds, diffusivity
    )

    pairs = [exchange(part, "tile", 1) for part in parts]
    halos = []
    for pair in pairs:
        shape = (pair.shape[0], pair.shape[1], ROUNDS, *pair.shape[3:])
        onward = on_core(onward_kernel, numbers, [pair], pltpu.VMEM(shape, jnp.float32))
        halos.append(("relay", pair.shape[0], (pair, relay(onward, "tile"))))

    met = on_core(
        first_choice_kernel,
        numbers,
        [winds, wind_other, diffusivity, diffusion_other],
        pltpu.VMEM((3, half, height, width), jnp.float32),
    )
    bit = 2
    while 2 * bit < groups:
        met = on_core(
            functools.partial(next_choice_kernel, bit),
            numbers,
            [met, exchange(met, "group", bit)],
            pltpu.VMEM(met.shape, jnp.float32),
        )
        bit *= 2
    with_winds = 2 * ROUNDS * (1 + WITH_WINDS)
    wind, wind_pair, wind_far, mix = on_core(
        functools.partial(last_choice_kernel, bit),
        numbers,
        [met, exchange(met, "group", bit), pair_first, far_first],
        [
            pltpu.VMEM((2, height, half, width), jnp.float32),
            pltpu.VMEM((with_winds, half, width), jnp.float32),
            pltpu.VMEM((with_winds, half, width), jnp.float32),
            pltpu.VMEM((half, height, width), jnp.float32),
        ],
    )
    wind_pair, wind_far = exchange(wind_pair, "tile", 1), cross(wind_far, "tile")
    halos.append(("winds", WITH_WINDS, (wind_pair, wind_far)))
    halos.append(("straight", STRAIGHT, (exchange(to_pair, "tile", 1), cross(to_far, "tile"))))
    known = on_core(
        gather_kernel,
        numbers,
        [wind, wind_pair, wind_far, mix],
        [pltpu.VMEM((height + 2 * ROUNDS + height // 2, half, width), jnp.float32)] * 2,
    )
    coef, solve = prepare(
        numbers, height, ROUNDS, [*known, *(exchange(x, "group", 1) for x in known)], []
    )

    result, start = None, 0
    for way, count, halo in halos:
        result = window(
            numbers, coef, solve, tracers, emissions, way, start, count, halo, result
        )
        start += count
    return result


def solution(mesh):
    return jax.shard_map(
        shards,
        mesh=mesh,
        in_specs=(
            P("group", None, "tile", None),
            P("group", "tile", None),
            P("group", None, None, "tile", None),
            P("group", None, "tile", None),
            P(),
            P(),
        ),
        out_specs=P("group", None, "tile", None),
        check_vma=False,
    )
```

```python
import functools

import jax
import jax.numpy as jnp
from jax import lax
from jax.experimental import pallas as pl
from jax.experimental.pallas import tpu as pltpu
from jax.sharding import PartitionSpec as P

ROUNDS = 6
DEEP = 8
RELAYED = (4,)
STRAIGHT = (3, 1)
ORDER = (0, 1, 2)
MIB = 1024 * 1024
VMEM_LIMIT = 32 * MIB
WINDOW_COST = 1
PREPARE_COST = 1


def exchange(value, axis, bit):
    count = lax.axis_size(axis)
    return lax.ppermute(value, axis, [(i, i ^ bit) for i in range(count)])


def cross(value, axis):
    count = lax.axis_size(axis)
    pairs = [(i, i + 1) for i in range(1, count - 1, 2)]
    return lax.ppermute(value, axis, pairs + [(j, i) for i, j in pairs])


def relay(value, axis):
    count = lax.axis_size(axis)
    pairs = [(i, i + 2) for i in range(0, count - 2, 2)] + [(i, i - 2) for i in range(3, count, 2)]
    return lax.ppermute(value, axis, pairs)


def in_smem(value):
    return pltpu.with_memory_space_constraint(value, pltpu.SMEM)


def in_vmem(values):
    return [pltpu.with_memory_space_constraint(value, pltpu.VMEM) for value in values]


def first_choice_kernel(numbers, wind, wind_other, diffusion, diffusion_other, *rest):
    out = rest[-1]
    slot, group = numbers[0], lax.axis_index("group")
    mine = slot % 2 == group % 2
    half = out.shape[1]
    base = group % 2 * half
    for k in range(half):
        for kind in range(2):
            out[kind, k] = jnp.where(mine, wind[0, kind, base + k], wind_other[0, kind, base + k])
        at = jnp.minimum(base + k, diffusion.shape[1] - 1)
        out[2, k] = jnp.where(mine, diffusion[0, at], diffusion_other[0, at])


def next_choice_kernel(bit, numbers, met, other, out):
    slot, group = numbers[0], lax.axis_index("group")
    out[...] = jnp.where((slot & bit) == (group & bit), met[...], other[...])


def last_choice_kernel(bit, numbers, met, other, *rest):
    wind, to_pair, to_far, mix = rest[-4:]
    group = lax.axis_index("group")
    mine = (numbers[0] & bit) == (group & bit)
    even = lax.axis_index("tile") % 2 == 0
    _, height, _, _ = wind.shape
    reach = to_pair.shape[1]
    for kind in range(2):
        rows = [
            jnp.where(mine, met[kind, :, j, :], other[kind, :, j, :]) for j in range(height)
        ]
        for j in range(height):
            wind[kind, j] = rows[j]
        for j in range(reach):
            last, first = rows[height - reach + j], rows[j]
            to_pair[kind, j] = jnp.where(even, last, first)
            to_far[kind, j] = jnp.where(even, first, last)
    mix[...] = jnp.where(mine, met[2], other[2])


def onward_kernel(_, pair, *rest):
    out = rest[-1]
    tracers, groups, reach = out.shape[:3]
    skip = jnp.where(lax.axis_index("tile") % 2 == 0, pair.shape[2] - reach, 0)
    for n in range(tracers):
        for g in range(groups):
            out[n, g] = pair[n, g, pl.ds(skip, reach)]


def pack_kernel(relayed, tiles, substeps_in, loader_in, tracers_in, wind_in, diffusion_in, *rest):
    numbers, tracers, wind, diffusion, *outs, substeps, loader, sem = rest
    copies = [
        pltpu.make_async_copy(source, target, sem.at[i])
        for i, (source, target) in enumerate(
            (
                (substeps_in, substeps),
                (loader_in, loader),
                (tracers_in, tracers),
                (wind_in, wind),
                (diffusion_in, diffusion),
            )
        )
    ]
    for copy in copies:
        copy.start()
    tile = lax.axis_index("tile")
    even = tile % 2 == 0
    _, levels, height, _ = tracers.shape
    straight = list(zip(outs[len(relayed) :: 2], outs[len(relayed) + 1 :: 2]))
    reach = outs[-1].shape[2]
    copies[2].wait()
    for g in range(levels // DEEP):
        deep = slice(g * DEEP, (g + 1) * DEEP)
        start = 0
        for part, count in zip(outs, relayed):
            for n in range(count):
                for j in range(height):
                    part[n, g, j] = tracers[start + n, deep, j, :]
            start += count
        for to_pair, to_far in straight:
            for n in range(to_pair.shape[0]):
                rows = [tracers[start + n, deep, j, :] for j in range(height)]
                for j in range(reach):
                    last, first = rows[height - reach + j], rows[j]
                    to_pair[n, g, j] = jnp.where(even, last, first)
                    to_far[n, g, j] = jnp.where(even, first, last)
            start += to_pair.shape[0]
    copies[0].wait()
    copies[1].wait()
    numbers[0] = loader[tile]
    numbers[1] = substeps[jnp.maximum(tile - 1, 0)]
    numbers[2] = substeps[tile]
    numbers[3] = substeps[jnp.minimum(tile + 1, tiles - 1)]
    copies[3].wait()
    copies[4].wait()


def pack(tiles, substeps, loader, tracers, winds, diffusivity):
    _, levels, height, width = tracers.shape

    def rows_of(count, rows):
        return pltpu.VMEM((count, levels // DEEP, rows, DEEP, width), jnp.float32)

    out_shape = [pltpu.SMEM((4,), jnp.int32)]
    out_shape += [pltpu.VMEM(x.shape, x.dtype) for x in (tracers, winds, diffusivity)]
    out_shape += [rows_of(count, height) for count in RELAYED]
    for count in STRAIGHT:
        out_shape += [rows_of(count, ROUNDS)] * 2
    vmem = pl.BlockSpec(memory_space=pltpu.VMEM)
    smem = pl.BlockSpec(memory_space=pltpu.SMEM)
    hbm = pl.BlockSpec(memory_space=pltpu.HBM)
    return pl.pallas_call(
        functools.partial(pack_kernel, RELAYED, tiles),
        out_shape=out_shape,
        in_specs=[hbm] * 5,
        out_specs=[smem] + [vmem] * (len(out_shape) - 1),
        scratch_shapes=[
            pltpu.SMEM(substeps.shape, jnp.int32),
            pltpu.SMEM(loader.shape, jnp.int32),
            pltpu.SemaphoreType.DMA((5,)),
        ],
        compiler_params=pltpu.CompilerParams(vmem_limit_bytes=VMEM_LIMIT),
        cost_estimate=pl.CostEstimate(flops=0, bytes_accessed=MIB, transcendentals=0),
    )(
        *[
            pltpu.with_memory_space_constraint(x, pltpu.HBM)
            for x in (substeps, loader, tracers, winds, diffusivity)
        ]
    )


def on_core(kernel, numbers, operands, out_shape, waits=(), cost=1):
    vmem = pl.BlockSpec(memory_space=pltpu.VMEM)
    return pl.pallas_call(
        kernel,
        out_shape=out_shape,
        in_specs=[pl.BlockSpec(memory_space=pltpu.SMEM)]
        + [vmem] * len(operands)
        + [pl.BlockSpec(memory_space=pl.ANY)] * len(waits),
        out_specs=jax.tree.map(lambda _: vmem, out_shape),
        compiler_params=pltpu.CompilerParams(vmem_limit_bytes=VMEM_LIMIT),
        cost_estimate=pl.CostEstimate(
            flops=0, bytes_accessed=cost * MIB, transcendentals=0
        ),
    )(in_smem(numbers), *in_vmem(operands), *waits)


def gather_kernel(_, wind, mix, pair, far, *rest):
    height = wind.shape[1]
    half = height // 2
    reach = pair.shape[1]
    even = lax.axis_index("tile") % 2 == 0
    pair_at = jnp.where(even, reach + height, 0)
    far_at = jnp.where(even, 0, reach + height)
    for kind, out in enumerate(rest[-2:]):
        out[pl.ds(pair_at, reach)] = pair[kind]
        out[pl.ds(reach, height)] = wind[kind]
        out[pl.ds(far_at, reach)] = far[kind]
        out[pl.ds(2 * reach + height, half)] = mix[pl.ds(kind * half, half)]


def prepare_kernel(height, reach, numbers, *rest):
    *blocks, coef, solve, faces, mixing = rest
    width = coef.shape[-1]
    groups = 2
    levels = groups * DEEP
    rows = height + 2 * reach
    half = height // 2
    tile, core = lax.axis_index("tile"), lax.axis_index("group") % 2
    for g, pair in ((core, blocks[:2]), (1 - core, blocks[2:4])):
        for kind, block in enumerate(pair):
            for j in range(rows):
                value = block[j]
                if kind == 1 and j == reach:
                    value = jnp.where(tile == 0, 0.0, value)
                faces[kind, g, height - reach + j] = value
            for k in range(half):
                mixing[g * DEEP + kind * half + k] = block[rows + k]
    counts = [numbers[t] for t in range(1, 4)]
    ones = jnp.ones((DEEP, width), jnp.float32)
    fractions = [ones / (ones * count.astype(jnp.float32)) for count in counts]
    reach -= 1
    for g in range(groups):
        for j in range(height - reach, 2 * height + reach):
            f = fractions[j // height]
            zonal, south, north = faces[0, g, j], faces[1, g, j], faces[1, g, j + 1]
            zonal_east = pltpu.roll(zonal, width - 1, 1)
            coef[g, j, 0] = 1.0 - f * (
                (jnp.maximum(zonal_east, 0.0) - jnp.minimum(zonal, 0.0))
                + (jnp.maximum(north, 0.0) - jnp.minimum(south, 0.0))
            )
            coef[g, j, 1] = f * jnp.maximum(zonal, 0.0)
            coef[g, j, 2] = -f * jnp.minimum(zonal_east, 0.0)
            coef[g, j, 3] = f * jnp.maximum(south, 0.0)
            coef[g, j, 4] = -f * jnp.minimum(north, 0.0)
    for j in range(height - reach, 2 * height + reach):
        coef[groups, j, 0] = ones
        for k in range(1, 5):
            coef[groups, j, k] = jnp.zeros_like(ones)
    ratio = lower = jnp.zeros((height, width), jnp.float32)
    for k in range(levels):
        upper = mixing[k] if k < levels - 1 else jnp.zeros_like(lower)
        pivot = 1.0 / (1.0 + lower + upper - lower * ratio)
        ratio = upper * pivot
        solve[k, 0] = lower
        solve[k, 1] = pivot
        solve[k, 2] = ratio
        lower = upper


def prepare(numbers, height, reach, blocks, waits):
    width = blocks[0].shape[-1]
    vmem = pl.BlockSpec(memory_space=pltpu.VMEM)
    return pl.pallas_call(
        functools.partial(prepare_kernel, height, reach),
        out_shape=(
            pltpu.VMEM((3, 3 * height, 5, DEEP, width), jnp.float32),
            pltpu.VMEM((2 * DEEP, 3, height, width), jnp.float32),
        ),
        in_specs=[pl.BlockSpec(memory_space=pltpu.SMEM)]
        + [vmem] * len(blocks)
        + [pl.BlockSpec(memory_space=pl.ANY)] * len(waits),
        out_specs=(vmem, vmem),
        scratch_shapes=[
            pltpu.VMEM((2, 2, 3 * height, DEEP, width), jnp.float32),
            pltpu.VMEM((2 * DEEP, height, width), jnp.float32),
        ],
        compiler_params=pltpu.CompilerParams(vmem_limit_bytes=VMEM_LIMIT),
        cost_estimate=pl.CostEstimate(
            flops=0, bytes_accessed=PREPARE_COST * MIB, transcendentals=0
        ),
    )(in_smem(numbers), *in_vmem(blocks), *waits)


def window_kernel(way, start, count, last, numbers, coef, solve, own, source, *rest):
    pair, far, *rest = rest
    if last:
        prior, out, field, advected, values, solved, sem = rest
        early = pltpu.make_async_copy(prior.at[:start], out.at[:start], sem.at[0])
        early.start()
    else:
        out, field, advected, values = rest[-4:]
    tracers = count
    reach = ROUNDS
    _, levels, height, width = own.shape
    groups = levels // DEEP
    tile = lax.axis_index("tile")
    even = tile % 2 == 0
    pair_at = jnp.where(even, 2 * height, 0 if way == "relay" else height - reach)
    far_at = jnp.where(even, height - reach, 2 * height)
    counts = [numbers[t] for t in range(1, 4)]
    for n in range(tracers):
        for g in range(groups):
            deep = slice(g * DEEP, (g + 1) * DEEP)
            for j in range(height):
                field[0, n, g, height + j] = own[start + n, deep, j, :]
            for j in range(reach):
                field[0, n, g, pair_at + j] = pair[n, g, j]
                field[0, n, g, far_at + j] = far[n, g, j]
            if way == "relay":
                for j in range(reach, height):
                    field[0, n, g, pair_at + j] = pair[n, g, j]
    for step in range(ROUNDS):
        reach = ROUNDS - 1 - step
        low, high = height - reach, 2 * height + reach
        src, dst = step % 2, (step + 1) % 2
        for g in range(groups):
            pages = [jnp.where(step < count, g, groups) for count in counts]
            south = [field[src, n, g, low - 1] for n in range(tracers)]
            here = [field[src, n, g, low] for n in range(tracers)]
            for j in range(low, high):
                c = [coef[pages[j // height], j, k] for k in range(5)]
                for n in range(tracers):
                    north = field[src, n, g, j + 1]
                    new = (
                        c[0] * here[n]
                        + c[1] * pltpu.roll(here[n], 1, 1)
                        + c[2] * pltpu.roll(here[n], width - 1, 1)
                        + c[3] * south[n]
                        + c[4] * north
                    )
                    if step < ROUNDS - 1:
                        field[dst, n, g, j] = new
                    else:
                        advected[n, g * DEEP : (g + 1) * DEEP, j - height, :] = new
                    south[n], here[n] = here[n], north
    for k in range(levels):
        lower, pivot = solve[k, 0], solve[k, 1]
        for n in range(tracers):
            q = advected[n, k]
            q = q + (source[start + n] if k == 0 else lower * values[n, k - 1])
            values[n, k] = q * pivot
    for n in range(tracers):
        target = solved.at[n] if last else out.at[start + n]
        current = values[n, levels - 1]
        target[levels - 1] = current
        for k in range(levels - 2, -1, -1):
            current = values[n, k] + solve[k, 2] * current
            target[k] = current
    if last:
        late = pltpu.make_async_copy(solved, out.at[start:], sem.at[1])
        late.start()
        early.wait()
        late.wait()


def window(numbers, coef, solve, tracers, emissions, way, start, count, halos, prior):
    total, levels, height, width = tracers.shape
    groups = levels // DEEP
    last = start + count == total
    vmem = pl.BlockSpec(memory_space=pltpu.VMEM)
    operands = [coef, solve, tracers, emissions, *halos]
    scratch = [
        pltpu.VMEM((2, count, groups, 3 * height, DEEP, width), jnp.float32),
        pltpu.VMEM((count, levels, height, width), jnp.float32),
        pltpu.VMEM((count, levels, height, width), jnp.float32),
    ]
    aliases = {}
    if prior is not None:
        operands.append(prior)
        if not last:
            aliases = {len(operands): 0}
    if last:
        scratch += [
            pltpu.VMEM((count, levels, height, width), jnp.float32),
            pltpu.SemaphoreType.DMA((2,)),
        ]
    shape = tracers.shape
    return pl.pallas_call(
        functools.partial(window_kernel, way, start, count, last),
        out_shape=jax.ShapeDtypeStruct(shape, jnp.float32)
        if last
        else pltpu.VMEM(shape, jnp.float32),
        in_specs=[pl.BlockSpec(memory_space=pltpu.SMEM)] + [vmem] * len(operands),
        out_specs=pl.BlockSpec(memory_space=pl.ANY) if last else vmem,
        scratch_shapes=scratch,
        input_output_aliases=aliases,
        compiler_params=pltpu.CompilerParams(vmem_limit_bytes=VMEM_LIMIT),
        cost_estimate=pl.CostEstimate(
            flops=0, bytes_accessed=WINDOW_COST * MIB, transcendentals=0
        ),
    )(in_smem(numbers), *in_vmem(operands))


def shards(tracers, emissions, winds, diffusivity, substeps, loader):
    tiles, groups = lax.axis_size("tile"), lax.axis_size("group")
    _, levels, height, width = tracers.shape
    half = levels // 2
    wind_other, diffusion_other = exchange(winds, "group", 1), exchange(diffusivity, "group", 1)
    numbers, tracers, winds, diffusivity, *parts = pack(
        tiles, substeps, loader, tracers, winds, diffusivity
    )

    parts, rows = parts[: len(RELAYED)], parts[len(RELAYED) :]
    pairs = [exchange(part, "tile", 1) for part in parts]
    straights = [
        (exchange(to_pair, "tile", 1), cross(to_far, "tile"))
        for to_pair, to_far in zip(rows[::2], rows[1::2])
    ]

    met = on_core(
        first_choice_kernel,
        numbers,
        [winds, wind_other, diffusivity, diffusion_other],
        pltpu.VMEM((3, half, height, width), jnp.float32),
    )
    bit = 2
    while 2 * bit < groups:
        met = on_core(
            functools.partial(next_choice_kernel, bit),
            numbers,
            [met, exchange(met, "group", bit)],
            pltpu.VMEM(met.shape, jnp.float32),
        )
        bit *= 2
    wind, wind_pair, wind_far, mix = on_core(
        functools.partial(last_choice_kernel, bit),
        numbers,
        [met, exchange(met, "group", bit)],
        [
            pltpu.VMEM((2, height, half, width), jnp.float32),
            pltpu.VMEM((2, ROUNDS, half, width), jnp.float32),
            pltpu.VMEM((2, ROUNDS, half, width), jnp.float32),
            pltpu.VMEM((half, height, width), jnp.float32),
        ],
    )
    wind_pair, wind_far = exchange(wind_pair, "tile", 1), cross(wind_far, "tile")
    halos, start = [], 0
    for pair in pairs:
        shape = (pair.shape[0], pair.shape[1], ROUNDS, *pair.shape[3:])
        onward = on_core(
            onward_kernel,
            numbers,
            [pair],
            pltpu.VMEM(shape, jnp.float32),
        )
        halos.append(("relay", start, (pair, relay(onward, "tile"))))
        start += pair.shape[0]
    start = sum(RELAYED)
    for halo in straights:
        halos.append(("straight", start, halo))
        start += halo[0].shape[0]
    known = on_core(
        gather_kernel,
        numbers,
        [wind, mix, wind_pair, wind_far],
        [pltpu.VMEM((height + 2 * ROUNDS + height // 2, half, width), jnp.float32)] * 2,
    )
    coef, solve = prepare(
        numbers, height, ROUNDS, [*known, *(exchange(x, "group", 1) for x in known)], []
    )

    result = None
    for way, start, halo in [halos[k] for k in ORDER]:
        count = halo[0].shape[0]
        result = window(
            numbers, coef, solve, tracers, emissions, way, start, count, halo, result
        )
    return result


def solution(mesh):
    return jax.shard_map(
        shards,
        mesh=mesh,
        in_specs=(
            P("group", None, "tile", None),
            P("group", "tile", None),
            P("group", None, None, "tile", None),
            P("group", None, "tile", None),
            P(),
            P(),
        ),
        out_specs=P("group", None, "tile", None),
        check_vma=False,
    )
```

```python
import functools

import jax
import jax.numpy as jnp
from jax import lax
from jax.experimental import pallas as pl
from jax.experimental.pallas import tpu as pltpu
from jax.sharding import PartitionSpec as P

ROUNDS = 6
DEEP = 8
RELAYED = (4,)
STRAIGHT = (3, 1)
ORDER = (0, 1, 2)
MIB = 1024 * 1024
VMEM_LIMIT = 32 * MIB
WINDOW_COST = 1
PREPARE_COST = 1


def exchange(value, axis, bit):
    count = lax.axis_size(axis)
    return lax.ppermute(value, axis, [(i, i ^ bit) for i in range(count)])


def cross(value, axis):
    count = lax.axis_size(axis)
    pairs = [(i, i + 1) for i in range(1, count - 1, 2)]
    return lax.ppermute(value, axis, pairs + [(j, i) for i, j in pairs])


def relay(value, axis):
    count = lax.axis_size(axis)
    pairs = [(i, i + 2) for i in range(0, count - 2, 2)] + [(i, i - 2) for i in range(3, count, 2)]
    return lax.ppermute(value, axis, pairs)


def in_smem(value):
    return pltpu.with_memory_space_constraint(value, pltpu.SMEM)


def in_vmem(values):
    return [pltpu.with_memory_space_constraint(value, pltpu.VMEM) for value in values]


def first_choice_kernel(numbers, wind, wind_other, diffusion, diffusion_other, *rest):
    out = rest[-1]
    slot, group = numbers[0], lax.axis_index("group")
    mine = slot % 2 == group % 2
    half = out.shape[1]
    base = group % 2 * half
    for k in range(half):
        for kind in range(2):
            out[kind, k] = jnp.where(mine, wind[0, kind, base + k], wind_other[0, kind, base + k])
        at = jnp.minimum(base + k, diffusion.shape[1] - 1)
        out[2, k] = jnp.where(mine, diffusion[0, at], diffusion_other[0, at])


def next_choice_kernel(bit, numbers, met, other, out):
    slot, group = numbers[0], lax.axis_index("group")
    out[...] = jnp.where((slot & bit) == (group & bit), met[...], other[...])


def last_choice_kernel(bit, numbers, met, other, *rest):
    wind, to_pair, to_far, mix = rest[-4:]
    group = lax.axis_index("group")
    mine = (numbers[0] & bit) == (group & bit)
    even = lax.axis_index("tile") % 2 == 0
    _, height, _, _ = wind.shape
    reach = to_pair.shape[1]
    for kind in range(2):
        rows = [
            jnp.where(mine, met[kind, :, j, :], other[kind, :, j, :]) for j in range(height)
        ]
        for j in range(height):
            wind[kind, j] = rows[j]
        for j in range(reach):
            last, first = rows[height - reach + j], rows[j]
            to_pair[kind, j] = jnp.where(even, last, first)
            to_far[kind, j] = jnp.where(even, first, last)
    mix[...] = jnp.where(mine, met[2], other[2])


def onward_kernel(_, pair, *rest):
    out = rest[-1]
    tracers, groups, reach = out.shape[:3]
    skip = jnp.where(lax.axis_index("tile") % 2 == 0, pair.shape[2] - reach, 0)
    for n in range(tracers):
        for g in range(groups):
            out[n, g] = pair[n, g, pl.ds(skip, reach)]


def pack_kernel(relayed, tiles, substeps_in, loader_in, tracers_in, wind_in, diffusion_in, *rest):
    numbers, tracers, wind, diffusion, *outs, substeps, loader, sem = rest
    sources = [(tracers_in.at[n], tracers.at[n]) for n in range(tracers.shape[0])]
    sources += [
        (substeps_in, substeps),
        (loader_in, loader),
        (wind_in, wind),
        (diffusion_in, diffusion),
    ]
    copies = [
        pltpu.make_async_copy(source, target, sem.at[i])
        for i, (source, target) in enumerate(sources)
    ]
    for copy in copies:
        copy.start()
    tile = lax.axis_index("tile")
    even = tile % 2 == 0
    _, levels, height, _ = tracers.shape
    straight = list(zip(outs[len(relayed) :: 2], outs[len(relayed) + 1 :: 2]))
    reach = outs[-1].shape[2]
    start = 0
    for part, count in zip(outs, relayed):
        for n in range(count):
            copies[start + n].wait()
            for g in range(levels // DEEP):
                for j in range(height):
                    part[n, g, j] = tracers[start + n, g * DEEP : (g + 1) * DEEP, j, :]
        start += count
    for to_pair, to_far in straight:
        for n in range(to_pair.shape[0]):
            copies[start + n].wait()
            for g in range(levels // DEEP):
                deep = slice(g * DEEP, (g + 1) * DEEP)
                rows = [tracers[start + n, deep, j, :] for j in range(height)]
                for j in range(reach):
                    last, first = rows[height - reach + j], rows[j]
                    to_pair[n, g, j] = jnp.where(even, last, first)
                    to_far[n, g, j] = jnp.where(even, first, last)
        start += to_pair.shape[0]
    for copy in copies[start:]:
        copy.wait()
    numbers[0] = loader[tile]
    numbers[1] = substeps[jnp.maximum(tile - 1, 0)]
    numbers[2] = substeps[tile]
    numbers[3] = substeps[jnp.minimum(tile + 1, tiles - 1)]


def pack(tiles, substeps, loader, tracers, winds, diffusivity):
    _, levels, height, width = tracers.shape

    def rows_of(count, rows):
        return pltpu.VMEM((count, levels // DEEP, rows, DEEP, width), jnp.float32)

    out_shape = [pltpu.SMEM((4,), jnp.int32)]
    out_shape += [pltpu.VMEM(x.shape, x.dtype) for x in (tracers, winds, diffusivity)]
    out_shape += [rows_of(count, height) for count in RELAYED]
    for count in STRAIGHT:
        out_shape += [rows_of(count, ROUNDS)] * 2
    vmem = pl.BlockSpec(memory_space=pltpu.VMEM)
    smem = pl.BlockSpec(memory_space=pltpu.SMEM)
    hbm = pl.BlockSpec(memory_space=pltpu.HBM)
    return pl.pallas_call(
        functools.partial(pack_kernel, RELAYED, tiles),
        out_shape=out_shape,
        in_specs=[hbm] * 5,
        out_specs=[smem] + [vmem] * (len(out_shape) - 1),
        scratch_shapes=[
            pltpu.SMEM(substeps.shape, jnp.int32),
            pltpu.SMEM(loader.shape, jnp.int32),
            pltpu.SemaphoreType.DMA((tracers.shape[0] + 4,)),
        ],
        compiler_params=pltpu.CompilerParams(vmem_limit_bytes=VMEM_LIMIT),
        cost_estimate=pl.CostEstimate(flops=0, bytes_accessed=MIB, transcendentals=0),
    )(
        *[
            pltpu.with_memory_space_constraint(x, pltpu.HBM)
            for x in (substeps, loader, tracers, winds, diffusivity)
        ]
    )


def on_core(kernel, numbers, operands, out_shape, waits=(), cost=1):
    vmem = pl.BlockSpec(memory_space=pltpu.VMEM)
    return pl.pallas_call(
        kernel,
        out_shape=out_shape,
        in_specs=[pl.BlockSpec(memory_space=pltpu.SMEM)]
        + [vmem] * len(operands)
        + [pl.BlockSpec(memory_space=pl.ANY)] * len(waits),
        out_specs=jax.tree.map(lambda _: vmem, out_shape),
        compiler_params=pltpu.CompilerParams(vmem_limit_bytes=VMEM_LIMIT),
        cost_estimate=pl.CostEstimate(
            flops=0, bytes_accessed=cost * MIB, transcendentals=0
        ),
    )(in_smem(numbers), *in_vmem(operands), *waits)


def gather_kernel(_, wind, mix, pair, far, *rest):
    height = wind.shape[1]
    half = height // 2
    reach = pair.shape[1]
    even = lax.axis_index("tile") % 2 == 0
    pair_at = jnp.where(even, reach + height, 0)
    far_at = jnp.where(even, 0, reach + height)
    for kind, out in enumerate(rest[-2:]):
        out[pl.ds(pair_at, reach)] = pair[kind]
        out[pl.ds(reach, height)] = wind[kind]
        out[pl.ds(far_at, reach)] = far[kind]
        out[pl.ds(2 * reach + height, half)] = mix[pl.ds(kind * half, half)]


def prepare_kernel(height, reach, numbers, *rest):
    *blocks, coef, solve, faces, mixing = rest
    width = coef.shape[-1]
    groups = 2
    levels = groups * DEEP
    rows = height + 2 * reach
    half = height // 2
    tile, core = lax.axis_index("tile"), lax.axis_index("group") % 2
    for g, pair in ((core, blocks[:2]), (1 - core, blocks[2:4])):
        for kind, block in enumerate(pair):
            for j in range(rows):
                value = block[j]
                if kind == 1 and j == reach:
                    value = jnp.where(tile == 0, 0.0, value)
                faces[kind, g, height - reach + j] = value
            for k in range(half):
                mixing[g * DEEP + kind * half + k] = block[rows + k]
    counts = [numbers[t] for t in range(1, 4)]
    ones = jnp.ones((DEEP, width), jnp.float32)
    fractions = [ones / (ones * count.astype(jnp.float32)) for count in counts]
    reach -= 1
    for g in range(groups):
        for j in range(height - reach, 2 * height + reach):
            f = fractions[j // height]
            zonal, south, north = faces[0, g, j], faces[1, g, j], faces[1, g, j + 1]
            zonal_east = pltpu.roll(zonal, width - 1, 1)
            coef[g, j, 0] = 1.0 - f * (
                (jnp.maximum(zonal_east, 0.0) - jnp.minimum(zonal, 0.0))
                + (jnp.maximum(north, 0.0) - jnp.minimum(south, 0.0))
            )
            coef[g, j, 1] = f * jnp.maximum(zonal, 0.0)
            coef[g, j, 2] = -f * jnp.minimum(zonal_east, 0.0)
            coef[g, j, 3] = f * jnp.maximum(south, 0.0)
            coef[g, j, 4] = -f * jnp.minimum(north, 0.0)
    for j in range(height - reach, 2 * height + reach):
        coef[groups, j, 0] = ones
        for k in range(1, 5):
            coef[groups, j, k] = jnp.zeros_like(ones)
    ratio = lower = jnp.zeros((height, width), jnp.float32)
    for k in range(levels):
        upper = mixing[k] if k < levels - 1 else jnp.zeros_like(lower)
        pivot = 1.0 / (1.0 + lower + upper - lower * ratio)
        ratio = upper * pivot
        solve[k, 0] = lower
        solve[k, 1] = pivot
        solve[k, 2] = ratio
        lower = upper


def prepare(numbers, height, reach, blocks, waits):
    width = blocks[0].shape[-1]
    vmem = pl.BlockSpec(memory_space=pltpu.VMEM)
    return pl.pallas_call(
        functools.partial(prepare_kernel, height, reach),
        out_shape=(
            pltpu.VMEM((3, 3 * height, 5, DEEP, width), jnp.float32),
            pltpu.VMEM((2 * DEEP, 3, height, width), jnp.float32),
        ),
        in_specs=[pl.BlockSpec(memory_space=pltpu.SMEM)]
        + [vmem] * len(blocks)
        + [pl.BlockSpec(memory_space=pl.ANY)] * len(waits),
        out_specs=(vmem, vmem),
        scratch_shapes=[
            pltpu.VMEM((2, 2, 3 * height, DEEP, width), jnp.float32),
            pltpu.VMEM((2 * DEEP, height, width), jnp.float32),
        ],
        compiler_params=pltpu.CompilerParams(vmem_limit_bytes=VMEM_LIMIT),
        cost_estimate=pl.CostEstimate(
            flops=0, bytes_accessed=PREPARE_COST * MIB, transcendentals=0
        ),
    )(in_smem(numbers), *in_vmem(blocks), *waits)


def window_kernel(way, start, count, last, numbers, coef, solve, own, source, *rest):
    pair, far, *rest = rest
    if last:
        prior, out, field, advected, values, solved, sem = rest
        early = pltpu.make_async_copy(prior.at[:start], out.at[:start], sem.at[0])
        early.start()
    else:
        out, field, advected, values = rest[-4:]
    tracers = count
    reach = ROUNDS
    _, levels, height, width = own.shape
    groups = levels // DEEP
    tile = lax.axis_index("tile")
    even = tile % 2 == 0
    pair_at = jnp.where(even, 2 * height, 0 if way == "relay" else height - reach)
    far_at = jnp.where(even, height - reach, 2 * height)
    counts = [numbers[t] for t in range(1, 4)]
    for n in range(tracers):
        for g in range(groups):
            deep = slice(g * DEEP, (g + 1) * DEEP)
            for j in range(height):
                field[0, n, g, height + j] = own[start + n, deep, j, :]
            for j in range(reach):
                field[0, n, g, pair_at + j] = pair[n, g, j]
                field[0, n, g, far_at + j] = far[n, g, j]
            if way == "relay":
                for j in range(reach, height):
                    field[0, n, g, pair_at + j] = pair[n, g, j]
    for step in range(ROUNDS):
        reach = ROUNDS - 1 - step
        low, high = height - reach, 2 * height + reach
        src, dst = step % 2, (step + 1) % 2
        for g in range(groups):
            pages = [jnp.where(step < count, g, groups) for count in counts]
            south = [field[src, n, g, low - 1] for n in range(tracers)]
            here = [field[src, n, g, low] for n in range(tracers)]
            for j in range(low, high):
                c = [coef[pages[j // height], j, k] for k in range(5)]
                for n in range(tracers):
                    north = field[src, n, g, j + 1]
                    new = (
                        c[0] * here[n]
                        + c[1] * pltpu.roll(here[n], 1, 1)
                        + c[2] * pltpu.roll(here[n], width - 1, 1)
                        + c[3] * south[n]
                        + c[4] * north
                    )
                    if step < ROUNDS - 1:
                        field[dst, n, g, j] = new
                    else:
                        advected[n, g * DEEP : (g + 1) * DEEP, j - height, :] = new
                    south[n], here[n] = here[n], north
    for k in range(levels):
        lower, pivot = solve[k, 0], solve[k, 1]
        for n in range(tracers):
            q = advected[n, k]
            q = q + (source[start + n] if k == 0 else lower * values[n, k - 1])
            values[n, k] = q * pivot
    for n in range(tracers):
        target = solved.at[n] if last else out.at[start + n]
        current = values[n, levels - 1]
        target[levels - 1] = current
        for k in range(levels - 2, -1, -1):
            current = values[n, k] + solve[k, 2] * current
            target[k] = current
    if last:
        late = pltpu.make_async_copy(solved, out.at[start:], sem.at[1])
        late.start()
        early.wait()
        late.wait()


def window(numbers, coef, solve, tracers, emissions, way, start, count, halos, prior):
    total, levels, height, width = tracers.shape
    groups = levels // DEEP
    last = start + count == total
    vmem = pl.BlockSpec(memory_space=pltpu.VMEM)
    operands = [coef, solve, tracers, emissions, *halos]
    scratch = [
        pltpu.VMEM((2, count, groups, 3 * height, DEEP, width), jnp.float32),
        pltpu.VMEM((count, levels, height, width), jnp.float32),
        pltpu.VMEM((count, levels, height, width), jnp.float32),
    ]
    aliases = {}
    if prior is not None:
        operands.append(prior)
        if not last:
            aliases = {len(operands): 0}
    if last:
        scratch += [
            pltpu.VMEM((count, levels, height, width), jnp.float32),
            pltpu.SemaphoreType.DMA((2,)),
        ]
    shape = tracers.shape
    return pl.pallas_call(
        functools.partial(window_kernel, way, start, count, last),
        out_shape=jax.ShapeDtypeStruct(shape, jnp.float32)
        if last
        else pltpu.VMEM(shape, jnp.float32),
        in_specs=[pl.BlockSpec(memory_space=pltpu.SMEM)] + [vmem] * len(operands),
        out_specs=pl.BlockSpec(memory_space=pl.ANY) if last else vmem,
        scratch_shapes=scratch,
        input_output_aliases=aliases,
        compiler_params=pltpu.CompilerParams(vmem_limit_bytes=VMEM_LIMIT),
        cost_estimate=pl.CostEstimate(
            flops=0, bytes_accessed=WINDOW_COST * MIB, transcendentals=0
        ),
    )(in_smem(numbers), *in_vmem(operands))


def shards(tracers, emissions, winds, diffusivity, substeps, loader):
    tiles, groups = lax.axis_size("tile"), lax.axis_size("group")
    _, levels, height, width = tracers.shape
    half = levels // 2
    wind_other, diffusion_other = exchange(winds, "group", 1), exchange(diffusivity, "group", 1)
    numbers, tracers, winds, diffusivity, *parts = pack(
        tiles, substeps, loader, tracers, winds, diffusivity
    )

    parts, rows = parts[: len(RELAYED)], parts[len(RELAYED) :]
    pairs = [exchange(part, "tile", 1) for part in parts]
    straights = [
        (exchange(to_pair, "tile", 1), cross(to_far, "tile"))
        for to_pair, to_far in zip(rows[::2], rows[1::2])
    ]

    met = on_core(
        first_choice_kernel,
        numbers,
        [winds, wind_other, diffusivity, diffusion_other],
        pltpu.VMEM((3, half, height, width), jnp.float32),
    )
    bit = 2
    while 2 * bit < groups:
        met = on_core(
            functools.partial(next_choice_kernel, bit),
            numbers,
            [met, exchange(met, "group", bit)],
            pltpu.VMEM(met.shape, jnp.float32),
        )
        bit *= 2
    wind, wind_pair, wind_far, mix = on_core(
        functools.partial(last_choice_kernel, bit),
        numbers,
        [met, exchange(met, "group", bit)],
        [
            pltpu.VMEM((2, height, half, width), jnp.float32),
            pltpu.VMEM((2, ROUNDS, half, width), jnp.float32),
            pltpu.VMEM((2, ROUNDS, half, width), jnp.float32),
            pltpu.VMEM((half, height, width), jnp.float32),
        ],
    )
    wind_pair, wind_far = exchange(wind_pair, "tile", 1), cross(wind_far, "tile")
    halos, start = [], 0
    for pair in pairs:
        shape = (pair.shape[0], pair.shape[1], ROUNDS, *pair.shape[3:])
        onward = on_core(
            onward_kernel,
            numbers,
            [pair],
            pltpu.VMEM(shape, jnp.float32),
        )
        halos.append(("relay", start, (pair, relay(onward, "tile"))))
        start += pair.shape[0]
    start = sum(RELAYED)
    for halo in straights:
        halos.append(("straight", start, halo))
        start += halo[0].shape[0]
    known = on_core(
        gather_kernel,
        numbers,
        [wind, mix, wind_pair, wind_far],
        [pltpu.VMEM((height + 2 * ROUNDS + height // 2, half, width), jnp.float32)] * 2,
    )
    coef, solve = prepare(
        numbers, height, ROUNDS, [*known, *(exchange(x, "group", 1) for x in known)], []
    )

    result = None
    for way, start, halo in [halos[k] for k in ORDER]:
        count = halo[0].shape[0]
        result = window(
            numbers, coef, solve, tracers, emissions, way, start, count, halo, result
        )
    return result


def solution(mesh):
    return jax.shard_map(
        shards,
        mesh=mesh,
        in_specs=(
            P("group", None, "tile", None),
            P("group", "tile", None),
            P("group", None, None, "tile", None),
            P("group", None, "tile", None),
            P(),
            P(),
        ),
        out_specs=P("group", None, "tile", None),
        check_vma=False,
    )
```

```python
import functools

import jax
import jax.numpy as jnp
from jax import lax
from jax.experimental import pallas as pl
from jax.experimental.pallas import tpu as pltpu
from jax.sharding import PartitionSpec as P

ROUNDS = 6
DEEP = 8
RELAYED = (4,)
STRAIGHT = (3, 1)
ORDER = (0, 1, 2)
MIB = 1024 * 1024
VMEM_LIMIT = 32 * MIB
WINDOW_COST = 1
PREPARE_COST = 1


def exchange(value, axis, bit):
    count = lax.axis_size(axis)
    return lax.ppermute(value, axis, [(i, i ^ bit) for i in range(count)])


def cross(value, axis):
    count = lax.axis_size(axis)
    pairs = [(i, i + 1) for i in range(1, count - 1, 2)]
    return lax.ppermute(value, axis, pairs + [(j, i) for i, j in pairs])


def relay(value, axis):
    count = lax.axis_size(axis)
    pairs = [(i, i + 2) for i in range(0, count - 2, 2)] + [(i, i - 2) for i in range(3, count, 2)]
    return lax.ppermute(value, axis, pairs)


def in_smem(value):
    return pltpu.with_memory_space_constraint(value, pltpu.SMEM)


def in_vmem(values):
    return [pltpu.with_memory_space_constraint(value, pltpu.VMEM) for value in values]


def first_choice_kernel(numbers, wind, wind_other, diffusion, diffusion_other, *rest):
    out = rest[-1]
    slot, group = numbers[0], lax.axis_index("group")
    mine = slot % 2 == group % 2
    half = out.shape[1]
    base = group % 2 * half
    for k in range(half):
        for kind in range(2):
            out[kind, k] = jnp.where(mine, wind[0, kind, base + k], wind_other[0, kind, base + k])
        at = jnp.minimum(base + k, diffusion.shape[1] - 1)
        out[2, k] = jnp.where(mine, diffusion[0, at], diffusion_other[0, at])


def next_choice_kernel(bit, numbers, met, other, out):
    slot, group = numbers[0], lax.axis_index("group")
    out[...] = jnp.where((slot & bit) == (group & bit), met[...], other[...])


def last_choice_kernel(bit, numbers, met, other, *rest):
    wind, to_pair, to_far, mix = rest[-4:]
    group = lax.axis_index("group")
    mine = (numbers[0] & bit) == (group & bit)
    even = lax.axis_index("tile") % 2 == 0
    _, height, _, _ = wind.shape
    reach = to_pair.shape[1]
    for kind in range(2):
        rows = [
            jnp.where(mine, met[kind, :, j, :], other[kind, :, j, :]) for j in range(height)
        ]
        for j in range(height):
            wind[kind, j] = rows[j]
        for j in range(reach):
            last, first = rows[height - reach + j], rows[j]
            to_pair[kind, j] = jnp.where(even, last, first)
            to_far[kind, j] = jnp.where(even, first, last)
    mix[...] = jnp.where(mine, met[2], other[2])


def onward_kernel(_, pair, *rest):
    out = rest[-1]
    tracers, groups, reach = out.shape[:3]
    skip = jnp.where(lax.axis_index("tile") % 2 == 0, pair.shape[2] - reach, 0)
    for n in range(tracers):
        for g in range(groups):
            out[n, g] = pair[n, g, pl.ds(skip, reach)]


def pack_kernel(relayed, tiles, substeps_in, loader_in, tracers_in, wind_in, diffusion_in, *rest):
    numbers, tracers, wind, diffusion, *outs, substeps, loader, sem = rest
    copies = [
        pltpu.make_async_copy(source, target, sem.at[i])
        for i, (source, target) in enumerate(
            (
                (substeps_in, substeps),
                (loader_in, loader),
                (tracers_in, tracers),
                (wind_in, wind),
                (diffusion_in, diffusion),
            )
        )
    ]
    for copy in copies:
        copy.start()
    tile = lax.axis_index("tile")
    even = tile % 2 == 0
    _, levels, height, _ = tracers.shape
    straight = list(zip(outs[len(relayed) :: 2], outs[len(relayed) + 1 :: 2]))
    reach = outs[-1].shape[2]
    copies[2].wait()
    for g in range(levels // DEEP):
        deep = slice(g * DEEP, (g + 1) * DEEP)
        start = 0
        for part, count in zip(outs, relayed):
            for n in range(count):
                for j in range(height):
                    part[n, g, j] = tracers[start + n, deep, j, :]
            start += count
        for to_pair, to_far in straight:
            for n in range(to_pair.shape[0]):
                rows = [tracers[start + n, deep, j, :] for j in range(height)]
                for j in range(reach):
                    last, first = rows[height - reach + j], rows[j]
                    to_pair[n, g, j] = jnp.where(even, last, first)
                    to_far[n, g, j] = jnp.where(even, first, last)
            start += to_pair.shape[0]
    copies[0].wait()
    copies[1].wait()
    numbers[0] = loader[tile]
    numbers[1] = substeps[jnp.maximum(tile - 1, 0)]
    numbers[2] = substeps[tile]
    numbers[3] = substeps[jnp.minimum(tile + 1, tiles - 1)]
    copies[3].wait()
    copies[4].wait()


def pack(tiles, substeps, loader, tracers, winds, diffusivity):
    _, levels, height, width = tracers.shape

    def rows_of(count, rows):
        return pltpu.VMEM((count, levels // DEEP, rows, DEEP, width), jnp.float32)

    out_shape = [pltpu.SMEM((4,), jnp.int32)]
    out_shape += [pltpu.VMEM(x.shape, x.dtype) for x in (tracers, winds, diffusivity)]
    out_shape += [rows_of(count, height) for count in RELAYED]
    for count in STRAIGHT:
        out_shape += [rows_of(count, ROUNDS)] * 2
    vmem = pl.BlockSpec(memory_space=pltpu.VMEM)
    smem = pl.BlockSpec(memory_space=pltpu.SMEM)
    hbm = pl.BlockSpec(memory_space=pltpu.HBM)
    return pl.pallas_call(
        functools.partial(pack_kernel, RELAYED, tiles),
        out_shape=out_shape,
        in_specs=[hbm] * 5,
        out_specs=[smem] + [vmem] * (len(out_shape) - 1),
        scratch_shapes=[
            pltpu.SMEM(substeps.shape, jnp.int32),
            pltpu.SMEM(loader.shape, jnp.int32),
            pltpu.SemaphoreType.DMA((5,)),
        ],
        compiler_params=pltpu.CompilerParams(vmem_limit_bytes=VMEM_LIMIT),
        cost_estimate=pl.CostEstimate(flops=0, bytes_accessed=MIB, transcendentals=0),
    )(
        *[
            pltpu.with_memory_space_constraint(x, pltpu.HBM)
            for x in (substeps, loader, tracers, winds, diffusivity)
        ]
    )


def on_core(kernel, numbers, operands, out_shape, waits=(), cost=1):
    vmem = pl.BlockSpec(memory_space=pltpu.VMEM)
    return pl.pallas_call(
        kernel,
        out_shape=out_shape,
        in_specs=[pl.BlockSpec(memory_space=pltpu.SMEM)]
        + [vmem] * len(operands)
        + [pl.BlockSpec(memory_space=pl.ANY)] * len(waits),
        out_specs=jax.tree.map(lambda _: vmem, out_shape),
        compiler_params=pltpu.CompilerParams(vmem_limit_bytes=VMEM_LIMIT),
        cost_estimate=pl.CostEstimate(
            flops=0, bytes_accessed=cost * MIB, transcendentals=0
        ),
    )(in_smem(numbers), *in_vmem(operands), *waits)


def gather_kernel(_, wind, mix, pair, far, *rest):
    height = wind.shape[1]
    half = height // 2
    reach = pair.shape[1]
    even = lax.axis_index("tile") % 2 == 0
    pair_at = jnp.where(even, reach + height, 0)
    far_at = jnp.where(even, 0, reach + height)
    for kind, out in enumerate(rest[-2:]):
        out[pl.ds(pair_at, reach)] = pair[kind]
        out[pl.ds(reach, height)] = wind[kind]
        out[pl.ds(far_at, reach)] = far[kind]
        out[pl.ds(2 * reach + height, half)] = mix[pl.ds(kind * half, half)]


def prepare_kernel(height, reach, numbers, *rest):
    *blocks, coef, solve, faces, mixing = rest
    width = coef.shape[-1]
    groups = 2
    levels = groups * DEEP
    rows = height + 2 * reach
    half = height // 2
    tile, core = lax.axis_index("tile"), lax.axis_index("group") % 2
    for g, pair in ((core, blocks[:2]), (1 - core, blocks[2:4])):
        for kind, block in enumerate(pair):
            for j in range(rows):
                value = block[j]
                if kind == 1 and j == reach:
                    value = jnp.where(tile == 0, 0.0, value)
                faces[kind, g, height - reach + j] = value
            for k in range(half):
                mixing[g * DEEP + kind * half + k] = block[rows + k]
    counts = [numbers[t] for t in range(1, 4)]
    ones = jnp.ones((DEEP, width), jnp.float32)
    fractions = [ones / (ones * count.astype(jnp.float32)) for count in counts]
    reach -= 1
    for g in range(groups):
        for j in range(height - reach, 2 * height + reach):
            f = fractions[j // height]
            zonal, south, north = faces[0, g, j], faces[1, g, j], faces[1, g, j + 1]
            zonal_east = pltpu.roll(zonal, width - 1, 1)
            coef[g, j, 0] = 1.0 - f * (
                (jnp.maximum(zonal_east, 0.0) - jnp.minimum(zonal, 0.0))
                + (jnp.maximum(north, 0.0) - jnp.minimum(south, 0.0))
            )
            coef[g, j, 1] = f * jnp.maximum(zonal, 0.0)
            coef[g, j, 2] = -f * jnp.minimum(zonal_east, 0.0)
            coef[g, j, 3] = f * jnp.maximum(south, 0.0)
            coef[g, j, 4] = -f * jnp.minimum(north, 0.0)
    for j in range(height - reach, 2 * height + reach):
        coef[groups, j, 0] = ones
        for k in range(1, 5):
            coef[groups, j, k] = jnp.zeros_like(ones)
    ratio = lower = jnp.zeros((height, width), jnp.float32)
    for k in range(levels):
        upper = mixing[k] if k < levels - 1 else jnp.zeros_like(lower)
        pivot = 1.0 / (1.0 + lower + upper - lower * ratio)
        ratio = upper * pivot
        solve[k, 0] = lower
        solve[k, 1] = pivot
        solve[k, 2] = ratio
        lower = upper


def prepare(numbers, height, reach, blocks, waits):
    width = blocks[0].shape[-1]
    vmem = pl.BlockSpec(memory_space=pltpu.VMEM)
    return pl.pallas_call(
        functools.partial(prepare_kernel, height, reach),
        out_shape=(
            pltpu.VMEM((3, 3 * height, 5, DEEP, width), jnp.float32),
            pltpu.VMEM((2 * DEEP, 3, height, width), jnp.float32),
        ),
        in_specs=[pl.BlockSpec(memory_space=pltpu.SMEM)]
        + [vmem] * len(blocks)
        + [pl.BlockSpec(memory_space=pl.ANY)] * len(waits),
        out_specs=(vmem, vmem),
        scratch_shapes=[
            pltpu.VMEM((2, 2, 3 * height, DEEP, width), jnp.float32),
            pltpu.VMEM((2 * DEEP, height, width), jnp.float32),
        ],
        compiler_params=pltpu.CompilerParams(vmem_limit_bytes=VMEM_LIMIT),
        cost_estimate=pl.CostEstimate(
            flops=0, bytes_accessed=PREPARE_COST * MIB, transcendentals=0
        ),
    )(in_smem(numbers), *in_vmem(blocks), *waits)


def window_kernel(way, start, count, last, numbers, coef, solve, own, source, *rest):
    pair, far, *rest = rest
    if last:
        prior, out, field, advected, values, solved, sem = rest
        early = pltpu.make_async_copy(prior.at[:start], out.at[:start], sem.at[0])
        early.start()
    else:
        out, field, advected, values = rest[-4:]
    tracers = count
    reach = ROUNDS
    _, levels, height, width = own.shape
    groups = levels // DEEP
    tile = lax.axis_index("tile")
    even = tile % 2 == 0
    pair_at = jnp.where(even, 2 * height, 0 if way == "relay" else height - reach)
    far_at = jnp.where(even, height - reach, 2 * height)
    counts = [numbers[t] for t in range(1, 4)]
    for n in range(tracers):
        for g in range(groups):
            deep = slice(g * DEEP, (g + 1) * DEEP)
            for j in range(height):
                field[0, n, g, height + j] = own[start + n, deep, j, :]
            for j in range(reach):
                field[0, n, g, pair_at + j] = pair[n, g, j]
                field[0, n, g, far_at + j] = far[n, g, j]
            if way == "relay":
                for j in range(reach, height):
                    field[0, n, g, pair_at + j] = pair[n, g, j]
    for step in range(ROUNDS):
        reach = ROUNDS - 1 - step
        low, high = height - reach, 2 * height + reach
        src, dst = step % 2, (step + 1) % 2
        for g in range(groups):
            pages = [jnp.where(step < count, g, groups) for count in counts]
            south = [field[src, n, g, low - 1] for n in range(tracers)]
            here = [field[src, n, g, low] for n in range(tracers)]
            for j in range(low, high):
                c = [coef[pages[j // height], j, k] for k in range(5)]
                for n in range(tracers):
                    north = field[src, n, g, j + 1]
                    new = (
                        c[0] * here[n]
                        + c[1] * pltpu.roll(here[n], 1, 1)
                        + c[2] * pltpu.roll(here[n], width - 1, 1)
                        + c[3] * south[n]
                        + c[4] * north
                    )
                    if step < ROUNDS - 1:
                        field[dst, n, g, j] = new
                    else:
                        advected[n, g * DEEP : (g + 1) * DEEP, j - height, :] = new
                    south[n], here[n] = here[n], north
    for k in range(levels):
        lower, pivot = solve[k, 0], solve[k, 1]
        for n in range(tracers):
            q = advected[n, k]
            q = q + (source[start + n] if k == 0 else lower * values[n, k - 1])
            values[n, k] = q * pivot
    late = []
    for n in range(tracers):
        target = solved.at[n] if last else out.at[start + n]
        current = values[n, levels - 1]
        target[levels - 1] = current
        for k in range(levels - 2, -1, -1):
            current = values[n, k] + solve[k, 2] * current
            target[k] = current
            if last and k in (levels // 2, 0):
                done = pl.ds(k, levels // 2)
                late.append(
                    pltpu.make_async_copy(
                        solved.at[n, done], out.at[start + n, done], sem.at[1 + len(late)]
                    )
                )
                late[-1].start()
    if last:
        early.wait()
        for copy in late:
            copy.wait()


def window(numbers, coef, solve, tracers, emissions, way, start, count, halos, prior):
    total, levels, height, width = tracers.shape
    groups = levels // DEEP
    last = start + count == total
    vmem = pl.BlockSpec(memory_space=pltpu.VMEM)
    operands = [coef, solve, tracers, emissions, *halos]
    scratch = [
        pltpu.VMEM((2, count, groups, 3 * height, DEEP, width), jnp.float32),
        pltpu.VMEM((count, levels, height, width), jnp.float32),
        pltpu.VMEM((count, levels, height, width), jnp.float32),
    ]
    aliases = {}
    if prior is not None:
        operands.append(prior)
        if not last:
            aliases = {len(operands): 0}
    if last:
        scratch += [
            pltpu.VMEM((count, levels, height, width), jnp.float32),
            pltpu.SemaphoreType.DMA((1 + 2 * count,)),
        ]
    shape = tracers.shape
    return pl.pallas_call(
        functools.partial(window_kernel, way, start, count, last),
        out_shape=jax.ShapeDtypeStruct(shape, jnp.float32)
        if last
        else pltpu.VMEM(shape, jnp.float32),
        in_specs=[pl.BlockSpec(memory_space=pltpu.SMEM)] + [vmem] * len(operands),
        out_specs=pl.BlockSpec(memory_space=pl.ANY) if last else vmem,
        scratch_shapes=scratch,
        input_output_aliases=aliases,
        compiler_params=pltpu.CompilerParams(vmem_limit_bytes=VMEM_LIMIT),
        cost_estimate=pl.CostEstimate(
            flops=0, bytes_accessed=WINDOW_COST * MIB, transcendentals=0
        ),
    )(in_smem(numbers), *in_vmem(operands))


def shards(tracers, emissions, winds, diffusivity, substeps, loader):
    tiles, groups = lax.axis_size("tile"), lax.axis_size("group")
    _, levels, height, width = tracers.shape
    half = levels // 2
    wind_other, diffusion_other = exchange(winds, "group", 1), exchange(diffusivity, "group", 1)
    numbers, tracers, winds, diffusivity, *parts = pack(
        tiles, substeps, loader, tracers, winds, diffusivity
    )

    parts, rows = parts[: len(RELAYED)], parts[len(RELAYED) :]
    pairs = [exchange(part, "tile", 1) for part in parts]
    straights = [
        (exchange(to_pair, "tile", 1), cross(to_far, "tile"))
        for to_pair, to_far in zip(rows[::2], rows[1::2])
    ]

    met = on_core(
        first_choice_kernel,
        numbers,
        [winds, wind_other, diffusivity, diffusion_other],
        pltpu.VMEM((3, half, height, width), jnp.float32),
    )
    bit = 2
    while 2 * bit < groups:
        met = on_core(
            functools.partial(next_choice_kernel, bit),
            numbers,
            [met, exchange(met, "group", bit)],
            pltpu.VMEM(met.shape, jnp.float32),
        )
        bit *= 2
    wind, wind_pair, wind_far, mix = on_core(
        functools.partial(last_choice_kernel, bit),
        numbers,
        [met, exchange(met, "group", bit)],
        [
            pltpu.VMEM((2, height, half, width), jnp.float32),
            pltpu.VMEM((2, ROUNDS, half, width), jnp.float32),
            pltpu.VMEM((2, ROUNDS, half, width), jnp.float32),
            pltpu.VMEM((half, height, width), jnp.float32),
        ],
    )
    wind_pair, wind_far = exchange(wind_pair, "tile", 1), cross(wind_far, "tile")
    halos, start = [], 0
    for pair in pairs:
        shape = (pair.shape[0], pair.shape[1], ROUNDS, *pair.shape[3:])
        onward = on_core(
            onward_kernel,
            numbers,
            [pair],
            pltpu.VMEM(shape, jnp.float32),
        )
        halos.append(("relay", start, (pair, relay(onward, "tile"))))
        start += pair.shape[0]
    start = sum(RELAYED)
    for halo in straights:
        halos.append(("straight", start, halo))
        start += halo[0].shape[0]
    known = on_core(
        gather_kernel,
        numbers,
        [wind, mix, wind_pair, wind_far],
        [pltpu.VMEM((height + 2 * ROUNDS + height // 2, half, width), jnp.float32)] * 2,
    )
    coef, solve = prepare(
        numbers, height, ROUNDS, [*known, *(exchange(x, "group", 1) for x in known)], []
    )

    result = None
    for way, start, halo in [halos[k] for k in ORDER]:
        count = halo[0].shape[0]
        result = window(
            numbers, coef, solve, tracers, emissions, way, start, count, halo, result
        )
    return result


def solution(mesh):
    return jax.shard_map(
        shards,
        mesh=mesh,
        in_specs=(
            P("group", None, "tile", None),
            P("group", "tile", None),
            P("group", None, None, "tile", None),
            P("group", None, "tile", None),
            P(),
            P(),
        ),
        out_specs=P("group", None, "tile", None),
        check_vma=False,
    )
```
